512 devices in a mesh: dp: 8 (over y, core), tensor: 64 (over x, z).
Axes of the slice: x: 4, y: 4, z: 16, core: 2. Of those that a mesh axis runs over, the one named last changes fastest.
Arguments:
- tokens: bfloat16 [1024, 8192], P('dp', 'tensor'), may hold values from -6 to 6
- grad_out: bfloat16 [1024, 8192], P('dp', 'tensor'), may hold values from -6 to 6
- up_weight: bfloat16 [64, 128, 4096], P('tensor', 'dp'), may hold values from -0.125 to 0.125
- down_weight: bfloat16 [64, 128, 4096], P('tensor', 'dp'), may hold values from -0.125 to 0.125
- up_local: int32 [64, 128], P('tensor'), may hold values from 0 to 3, as said below
- up_col: int32 [64, 128], P('tensor'), may hold values from 0 to 127, as said below
- down_local: int32 [64, 128], P('tensor'), may hold values from 0 to 3, as said below
- down_col: int32 [64, 128], P('tensor'), may hold values from 0 to 127, as said below
- up_perm: int32 [256], replicated, may hold values from 0 to 255, each once
- down_perm: int32 [256], replicated, may hold values from 0 to 255, each once
Outputs:
- grad_tokens: bfloat16 [1024, 8192], P('dp', 'tensor')
- grad_up: bfloat16 [64, 128, 4096], P('tensor')
- grad_down: bfloat16 [64, 128, 4096], P('tensor')
The draws below stay inside these ranges and needn't reach their ends.
Inputs may be any that keep to these rules, and one draw needn't show every extreme that they name: `up_local`: for each owner, slots of one hidden block stand together, blocks in rising order, each of its 4 blocks with one slot or more. `up_col`: input blocks of one hidden block are distinct. `down_local`: for each owner, slots of one hidden block stand together, blocks in rising order, each of its 4 blocks with one slot or more. `down_col`: output blocks of one hidden block are distinct.
All inputs are finite; a program needn't handle non-finite values.
Results may differ from the reference program's by a relative error of at most 0.017.
Values may be sent and summed in bfloat16 or wider, within the bound.
No kernel may reach another device: no remote copies, remote signals or barrier semaphores. Data moves between devices by JAX's collectives and lax.ppermute only.
A program may use at most 64 MiB of HBM per device.

```python
import math
import jax
import jax.numpy as jnp
from jax import lax

D = 8192
BLOCK = 64
HPD = 4
TOK = 128
DB = 128
KEEP = 32
SLOTS = 128
FB = 256
TOKENS = 1024
N_DP = 8
N_TENSOR = 64


def slot_tables(key):
    excess = jax.random.randint(jax.random.fold_in(key, 1), (N_TENSOR, HPD), 0, KEEP // 2 + 1)
    counts = KEEP + excess - jnp.roll(excess, -1, axis=1)
    ends = jnp.cumsum(counts, axis=1)
    starts = ends - counts
    slot_ids = jnp.arange(SLOTS, dtype=jnp.int32)
    local = jnp.sum((slot_ids[None, :, None] >= ends[:, None, :]).astype(jnp.int32), axis=2).astype(jnp.int32)
    offset = slot_ids[None, :] - jnp.take_along_axis(starts, local, axis=1)
    keys = jax.random.split(jax.random.fold_in(key, 2), N_TENSOR * HPD)
    orders = jax.vmap(lambda one: jax.random.permutation(one, DB))(keys).reshape(N_TENSOR, HPD, DB)
    owners = jnp.arange(N_TENSOR, dtype=jnp.int32)[:, None]
    cols = orders[owners, local, offset].astype(jnp.int32)
    return (local, cols)


def draw_up_local(key, part):
    local, cols = slot_tables(jax.random.fold_in(key, 21))
    return local


def draw_up_col(key, part):
    local, cols = slot_tables(jax.random.fold_in(key, 21))
    return cols


def draw_down_local(key, part):
    local, cols = slot_tables(jax.random.fold_in(key, 22))
    return local


def draw_down_col(key, part):
    local, cols = slot_tables(jax.random.fold_in(key, 22))
    return cols


def block_levels(stream_key, extent, shards, least, high):
    gain, own = 1.0, jax.random.fold_in(stream_key, 6)
    for axis_at, blocks in shards:
        heights = jnp.exp(jax.random.uniform(jax.random.fold_in(own, axis_at), (blocks,), jnp.float32, least / len(shards), high / len(shards)))
        gain = gain * jnp.repeat(heights, extent[axis_at] // blocks).reshape([-1 if axis == axis_at else 1 for axis in range(len(extent))])
    return gain


def noise(rng, extent, width, most, cuts=(), held_as=jnp.bfloat16):
    loudness = block_levels(rng, extent, cuts, -0.22, 0.18) if cuts else 1.0
    drawn = jax.random.normal(rng, extent, jnp.float32) * width * loudness
    return jnp.minimum(jnp.maximum(drawn, -most), most).astype(held_as)


def setup_inputs(seed: int = 0) -> dict:
    splits = jax.random.split(jax.random.key(seed), 11)
    tokens = noise(splits[0], (TOKENS, D), 1.0, 6.0, ((0, 8), (1, 64)))
    grad_out = noise(splits[1], (TOKENS, D), 1.0, 6.0, ((0, 8), (1, 64)))
    up_weight = noise(splits[2], (N_TENSOR, SLOTS, BLOCK * BLOCK), (KEEP * BLOCK) ** -0.5, 0.125, ((0, 64), (1, 8)))
    down_weight = noise(splits[3], (N_TENSOR, SLOTS, BLOCK * BLOCK), (KEEP * BLOCK) ** -0.5, 0.125, ((0, 64), (1, 8)))
    up_local = draw_up_local(jax.random.fold_in(splits[10], 71), 0)
    up_col = draw_up_col(jax.random.fold_in(splits[10], 71), 0)
    down_local = draw_down_local(jax.random.fold_in(splits[10], 71), 0)
    down_col = draw_down_col(jax.random.fold_in(splits[10], 71), 0)
    up_perm = jax.random.permutation(splits[8], FB).astype(jnp.int32)
    down_perm = jax.random.permutation(splits[9], FB).astype(jnp.int32)
    return {"tokens": tokens, "grad_out": grad_out, "up_weight": up_weight, "down_weight": down_weight, "up_local": up_local, "up_col": up_col, "down_local": down_local, "down_col": down_col, "up_perm": up_perm, "down_perm": down_perm}


def gelu_parts(value):
    cdf = 0.5 * (1.0 + lax.erf(value * 0.7071067811865476))
    return (value * cdf, cdf + value * jnp.exp(-0.5 * value * value) * 0.3989422804014327)

def settle(parts):
    rounded = lax.optimization_barrier(parts.astype(jnp.bfloat16)).astype(jnp.float32)
    return lax.optimization_barrier(jnp.sum(rounded, axis=0)).astype(jnp.bfloat16)

def reference(tokens, grad_out, up_weight, down_weight, up_local, up_col, down_local, down_col, up_perm, down_perm):
    high = lax.Precision.HIGHEST
    total = tokens.shape[0]
    scale = 1.0 / math.sqrt(TOKENS)
    x_blocks = tokens.astype(jnp.float32).reshape(total, DB, BLOCK)
    dy_blocks = grad_out.astype(jnp.float32).reshape(total, DB, BLOCK)
    up_mats = up_weight.astype(jnp.float32).reshape(N_TENSOR, SLOTS, BLOCK, BLOCK)
    down_mats = down_weight.astype(jnp.float32).reshape(N_TENSOR, SLOTS, BLOCK, BLOCK)

    def forward_owner(args):
        mats, local, cols = args
        gathered = x_blocks[:, cols]
        prod = jnp.einsum('tsk,skn->stn', gathered, mats, precision=high)
        return jax.ops.segment_sum(prod, local, num_segments=HPD)
    pre_up = lax.map(forward_owner, (up_mats, up_local, up_col)).reshape(FB, total, BLOCK)
    pre = jnp.zeros((FB, total, BLOCK), jnp.float32).at[up_perm].set(pre_up)
    active, slope = gelu_parts(pre)
    hidden = active.astype(jnp.bfloat16).astype(jnp.float32)

    def down_owner(args):
        mats, local, cols, owned = args
        mine = hidden[owned]
        gathered = dy_blocks[:, cols]
        dh_slots = jnp.einsum('tsn,skn->stk', gathered, mats, precision=high)
        dh_local = jax.ops.segment_sum(dh_slots, local, num_segments=HPD)
        slots_h = mine[local].reshape(SLOTS, N_DP, TOK, BLOCK)
        parts = jnp.einsum('sdtk,dtsn->dskn', slots_h, gathered.reshape(N_DP, TOK, SLOTS, BLOCK), precision=high) * scale
        return (dh_local.astype(jnp.bfloat16), settle(parts))
    dh_down, grad_down = lax.map(down_owner, (down_mats, down_local, down_col, down_perm.reshape(N_TENSOR, HPD)))
    dh = jnp.zeros((FB, total, BLOCK), jnp.bfloat16).at[down_perm].set(dh_down.reshape(FB, total, BLOCK))
    dpre = (dh.astype(jnp.float32) * slope).astype(jnp.bfloat16).astype(jnp.float32)

    def up_owner(carry, args):
        mats, local, cols, owned = args
        mine = dpre[owned][local]
        dx_slots = jnp.einsum('stn,skn->stk', mine, mats, precision=high)
        carry = carry + jax.ops.segment_sum(dx_slots, cols, num_segments=DB)
        gathered = x_blocks[:, cols].reshape(N_DP, TOK, SLOTS, BLOCK)
        parts = jnp.einsum('dtsk,sdtn->dskn', gathered, mine.reshape(SLOTS, N_DP, TOK, BLOCK), precision=high) * scale
        return (carry, settle(parts))
    dx_acc, grad_up = lax.scan(up_owner, jnp.zeros((DB, total, BLOCK), jnp.float32), (up_mats, up_local, up_col, up_perm.reshape(N_TENSOR, HPD)))
    grad_tokens = jnp.transpose(dx_acc, (1, 0, 2)).reshape(total, D).astype(jnp.bfloat16)
    return (grad_tokens, grad_up.reshape(N_TENSOR, SLOTS, BLOCK * BLOCK), grad_down.reshape(N_TENSOR, SLOTS, BLOCK * BLOCK))
```

```python
import jax
import jax.numpy as jnp
import numpy as np
from jax import lax
from jax.experimental import pallas as pl
from jax.experimental.pallas import tpu as pltpu
from jax.sharding import PartitionSpec as P

BLOCK = 64
HPD = 4
NX, NZ, NY = 4, 16, 4
BF = jnp.bfloat16
F32 = jnp.float32
VM = pl.BlockSpec(memory_space=pltpu.VMEM)
SM = pl.BlockSpec(memory_space=pltpu.SMEM)


def from_tensor(value, dx, dz):
    pairs = [
        (((x + dx) % NX) * NZ + (z + dz) % NZ, x * NZ + z) for x in range(NX) for z in range(NZ)
    ]
    return lax.ppermute(value, "tensor", pairs)


def from_y(value, dy):
    pairs = [(((y + dy) % NY) * 2 + c, y * 2 + c) for y in range(NY) for c in range(2)]
    return lax.ppermute(value, "dp", pairs)


def from_core(value):
    return lax.ppermute(value, "dp", [(d ^ 1, d) for d in range(2 * NY)])


def add(*parts):
    total = parts[0].astype(F32)
    for part in parts[1:]:
        total = total + part.astype(F32)
    return total.astype(BF)


Z_ORDER = (0, 5, 11, 1, 6, 12, 15, 4, 10, 2, 7, 13, 14, 3, 9, 8)
Z_SLOT = np.argsort(np.array(Z_ORDER)).astype(np.int32)


def gather_features(tokens, grad_out):
    own = jnp.stack([tokens, grad_out])[:, None]
    plus, minus = from_tensor(own, 0, 5), from_tensor(own, 0, -5)
    three = jnp.concatenate([own, plus, minus], axis=1)
    parts = [three] + [from_tensor(three, 0, dz) for dz in (1, -1, 2, -2)] + [from_tensor(plus, 0, 3)]
    x, dy = (jnp.concatenate([part[i] for part in parts]) for i in range(2))
    x_plus, dy_minus = from_tensor(x, 1, 0), from_tensor(dy, -1, 0)
    dy_plus, x_minus = from_tensor(dy, 1, 0), from_tensor(x, -1, 0)
    x_two, dy_two = from_tensor(x_plus, 1, 0), from_tensor(dy_minus, -1, 0)
    return (x, x_plus, x_two, x_minus, dy, dy_plus, dy_two, dy_minus), (plus, minus)


def block_place(cols):
    me = lax.axis_index("tensor")
    owner = cols // 2
    dx = (owner // NZ - me // NZ) % NX
    dz = (owner - me) % NZ
    slot = jnp.sum(jnp.where(dz[:, None] == jnp.arange(NZ), Z_SLOT[None], 0), axis=1)
    return ((dx * NZ + slot) * 2 + cols % 2).astype(jnp.int32)


def left_half():
    return lax.broadcasted_iota(jnp.int32, (BLOCK, 2 * BLOCK), 1) < BLOCK


def swap_halves(tile):
    return jnp.concatenate([tile[:, BLOCK:], tile[:, :BLOCK]], axis=1)


def spread_kernel(up_at, up_loc, down_at, down_loc, pairs, up_dense, down_dense):
    left = left_half()

    def clear(i, _):
        up_dense[pl.ds(2 * i, 2)] = jnp.zeros((2, 256, 128), BF)
        down_dense[pl.ds(2 * i, 2)] = jnp.zeros((2, 256, 128), BF)
        return 0

    lax.fori_loop(0, 32, clear, 0)

    def place(g, _):
        for p in range(8):
            for which, at_ref, loc_ref, dense in (
                (0, up_at, up_loc, up_dense),
                (1, down_at, down_loc, down_dense),
            ):
                tile = pairs[g, which, p]
                turned = swap_halves(tile)
                for side in range(2):
                    slot = g * 16 + side * 8 + p
                    at, loc = at_ref[slot], loc_ref[slot]
                    half = at % 2
                    view = dense.at[at // 2, pl.ds(pl.multiple_of(loc * BLOCK, BLOCK), BLOCK), :]
                    value = jnp.where(half == side, tile, turned)
                    view[...] = jnp.where(left == (half == 0), value, view[...])
        return 0

    lax.fori_loop(0, 8, place, 0)


def spread_weights(tables, pairs):
    shape = jax.ShapeDtypeStruct((64, 256, 128), BF)
    return pl.pallas_call(
        spread_kernel,
        in_specs=[SM] * 4 + [VM],
        out_specs=[VM, VM],
        out_shape=[shape, shape],
        compiler_params=pltpu.CompilerParams(vmem_limit_bytes=16 << 20),
        cost_estimate=pl.CostEstimate(flops=0, bytes_accessed=12 << 20, transcendentals=0),
        name="spread_weights",
    )(*tables, pairs)


def exchange_order(outward):
    row = lax.broadcasted_iota(jnp.int32, (512, 512), 0 if outward else 1)
    col = lax.broadcasted_iota(jnp.int32, (512, 512), 1 if outward else 0)
    return ((row % 8) * BLOCK + row // 8 == col).astype(F32).astype(BF)


def wide(ref, start, count):
    return jnp.concatenate([ref[start + i] for i in range(count)], axis=1)


def times_dense(features, dense):
    total = None
    for part in range(4):
        for first in (0, 8):
            term = lax.dot_general(
                wide(features[part], first, 8),
                wide(dense, part * 16 + first, 8),
                (((1,), (1,)), ((), ())),
                preferred_element_type=F32,
            )
            total = term if total is None else total + term
    return total


def forward_kernel(*refs):
    xs, dys, (up_dense, down_dense, out, slope) = refs[:4], refs[4:8], refs[8:]
    pre = times_dense(xs, up_dense)
    cdf = 0.5 * (1.0 + lax.erf(pre * 0.7071067811865476))
    slope[...] = cdf + pre * jnp.exp(-0.5 * pre * pre) * 0.3989422804014327
    hidden = (pre * cdf).astype(BF)
    both = jnp.concatenate([hidden, times_dense(dys, down_dense).astype(BF)], axis=1)
    out[...] = lax.dot_general(
        exchange_order(True), both, (((1,), (1,)), ((), ())), preferred_element_type=F32
    ).astype(BF)


def forward(features, up_dense, down_dense):
    return pl.pallas_call(
        forward_kernel,
        in_specs=[VM] * 10,
        out_specs=[VM, VM],
        out_shape=[
            jax.ShapeDtypeStruct((512, 128), BF),
            jax.ShapeDtypeStruct((128, 256), F32),
        ],
        compiler_params=pltpu.CompilerParams(vmem_limit_bytes=28 << 20),
        cost_estimate=pl.CostEstimate(flops=1 << 30, bytes_accessed=12 << 20, transcendentals=1 << 16),
        name="forward",
    )(*features, up_dense, down_dense)


def backward_kernel(me_ref, z_slot, up_at, up_loc, down_at, down_loc, *refs):
    xs, dys, (back, slope, up_w) = refs[:4], refs[4:8], refs[8:11]
    (same, other, near, to_plus, to_minus, later, up_dense, down_dense) = refs[11:]
    left = left_half()
    scale = 1.0 / 32.0
    both = jnp.dot(exchange_order(False), back[...], preferred_element_type=F32)
    hidden_t = both[:256].astype(BF)
    dpre_f32 = both[256:].T * slope[...]
    dpre = dpre_f32.astype(BF)
    dpre_t = dpre_f32.T.astype(BF)

    def terms(target, z, part):
        w = jnp.concatenate([up_w[part * NZ + z_slot[z + j]] for j in range(2)], axis=1)
        value = jnp.dot(dpre, w, preferred_element_type=F32).astype(BF)
        target[z] = value[:, :128]
        target[z + 1] = value[:, 128:]

    for z in range(0, NZ, 2):
        low = z < NZ // 2
        terms(to_plus, z, 2 if low else 1)
        terms(to_minus, z, 3 if low else 2)
        terms(later, z, 1 if low else 3)
        terms(near, z, 0)

    for part in range(4):

        def step(i, _, part=part):
            at = part * 16 + 2 * i
            for lhs, source, dense in ((dpre_t, xs, up_dense), (hidden_t, dys, down_dense)):
                value = jnp.dot(lhs, wide(source[part], 2 * i, 2), preferred_element_type=F32)
                value = (value * scale).astype(BF)
                dense[at] = value[:, :128]
                dense[at + 1] = value[:, 128:]
            return 0

        lax.fori_loop(0, 8, step, 0, unroll=2)
    me = me_ref[0]
    for dc, target in ((0, same), (1, other)):

        def pick(dy, _, dc=dc, target=target):
            first = ((((me // 2 + dy) % NY) * 2) + (me % 2 + dc) % 2) * 16
            for p in range(8):
                for which, at_ref, loc_ref, dense in (
                    (0, up_at, up_loc, up_dense),
                    (1, down_at, down_loc, down_dense),
                ):
                    sides = []
                    for side in range(2):
                        slot = first + side * 8 + p
                        at, loc = at_ref[slot], loc_ref[slot]
                        tile = dense[at // 2, pl.ds(pl.multiple_of(loc * BLOCK, BLOCK), BLOCK), :]
                        sides.append(jnp.where(at % 2 == side, tile, swap_halves(tile)))
                    target[dy, which, p] = jnp.where(left, sides[0], sides[1])
            return 0

        lax.fori_loop(0, 4, pick, 0)


def backward(me, z_slot, tables, features, back, slope, up_w):
    shape = jax.ShapeDtypeStruct((4, 2, 8, BLOCK, 128), BF)
    chunk = jax.ShapeDtypeStruct((NZ, 128, 128), BF)
    return pl.pallas_call(
        backward_kernel,
        in_specs=[SM] * 6 + [VM] * 11,
        out_specs=[VM] * 6,
        out_shape=[shape, shape, chunk, chunk, chunk, chunk],
        scratch_shapes=[pltpu.VMEM((64, 256, 128), BF), pltpu.VMEM((64, 256, 128), BF)],
        compiler_params=pltpu.CompilerParams(vmem_limit_bytes=32 << 20),
        cost_estimate=pl.CostEstimate(flops=3 << 29, bytes_accessed=14 << 20, transcendentals=0),
        name="backward",
    )(me, z_slot, *tables, *features, back, slope, up_w)


def pack(up, down):
    up = jnp.swapaxes(up.reshape(2, 8, BLOCK, BLOCK), 2, 3)
    slots = jnp.stack([up, down.reshape(2, 8, BLOCK, BLOCK)])
    return jnp.concatenate([slots[:, 0], slots[:, 1]], axis=3)


def unpack(pairs, turned=False):
    axis = 1 if turned else 2
    slots = jnp.concatenate(jnp.split(pairs, 2, axis=axis))
    return slots.reshape(16, BLOCK * BLOCK)


Y_GROUPS = [[y * 2 + c for y in range(NY)] for c in range(2)]
Z_GROUPS = [[x * NZ + z for z in range(NZ)] for x in range(NX)]


def exchange(rows):
    return lax.all_to_all(rows.reshape(64, 8, 128), "tensor", 0, 0, tiled=True).reshape(512, 128)


def reduce_all(same, other, near, to_plus, to_minus, later):
    half = NZ // 2
    order = lax.optimization_barrier
    got_plus, got_minus = from_tensor(to_plus, -1, 0), from_tensor(to_minus, 1, 0)
    total = add(same, from_core(other))
    y_plus, y_minus = jnp.stack([total[2, 0], total[1, 1]]), jnp.stack([total[2, 1], total[3, 0]])
    got_plus, got_minus, _, _ = order((got_plus, got_minus, y_plus, y_minus))
    on_plus, on_minus = add(later[:half], got_plus[:half]), add(later[half:], got_minus[half:])
    y_plus, y_minus = from_y(y_plus, -1), from_y(y_minus, 1)
    low, high = from_tensor(on_plus, -1, 0), from_tensor(on_minus, 1, 0)
    y_plus, y_minus, _, _ = order((y_plus, y_minus, on_plus, on_minus))
    on_down, on_up = add(total[3, 1], y_minus[0]), add(total[1, 0], y_plus[0])
    low, high, _, _ = order((low, high, on_down, on_up))
    on_down, on_up = order((from_y(on_down, 1), from_y(on_up, -1)))
    down = unpack(add(total[0, 1], y_plus[1], on_down))
    up = unpack(jnp.swapaxes(add(total[0, 0], on_up, y_minus[1]), 1, 2), True)
    low = add(near[:half], low, got_minus[:half])
    high = add(near[half:], got_plus[half:], high)
    column, own = order((jnp.concatenate([low, high]), jnp.stack([up, down])))
    mine = lax.all_gather(own, "dp", axis=0, axis_index_groups=Y_GROUPS)
    parts = lax.all_to_all(column, "tensor", 0, 0, tiled=True, axis_index_groups=Z_GROUPS)
    theirs = from_core(mine)
    even = lax.axis_index("dp") % 2 == 0
    up, down = (
        jnp.stack(
            [
                jnp.where(even, mine[:, i], theirs[:, i]),
                jnp.where(even, theirs[:, i], mine[:, i]),
            ],
            axis=1,
        ).reshape(1, 128, -1)
        for i in range(2)
    )
    return jnp.sum(parts.astype(F32), axis=0).astype(BF), up, down


def per_device(
    tokens,
    grad_out,
    up_weight,
    down_weight,
    up_local,
    up_col,
    down_local,
    down_col,
    up_perm,
    down_perm,
):
    features, first = gather_features(tokens, grad_out)
    up_own, down_own, *_ = lax.optimization_barrier((up_weight[0], down_weight[0], *first))
    pairs = lax.all_gather(pack(up_own, down_own), "dp", axis=0)
    tables = (block_place(up_col[0]), up_local[0], block_place(down_col[0]), down_local[0])
    up4, down4 = up_perm.reshape(-1, HPD), down_perm.reshape(-1, HPD)
    wanted = jnp.stack([down4, up4 + 256], axis=1).reshape(-1)
    present = jnp.stack([up4, down4 + 256], axis=1).reshape(-1)
    route = (wanted[:, None] == present[None, :]).astype(BF)
    z_from_me = (jnp.arange(NZ) - lax.axis_index("tensor")) % NZ
    z_slot = jnp.sum(jnp.where(z_from_me[:, None] == jnp.arange(NZ), Z_SLOT[None], 0), axis=1)

    up_dense, down_dense = spread_weights(tables, pairs)
    sent, slope = forward(features, up_dense, down_dense)
    routed = jnp.dot(route, exchange(sent), preferred_element_type=F32).astype(BF)
    back = exchange(routed)
    me = lax.axis_index("dp").astype(jnp.int32)
    terms = backward(
        me.reshape(1), z_slot.astype(jnp.int32), tables, features, back, slope, up_dense
    )
    return reduce_all(*terms)


def solution(mesh):
    return jax.shard_map(
        per_device,
        mesh=mesh,
        in_specs=(
            P("dp", "tensor"),
            P("dp", "tensor"),
            P("tensor", "dp", None),
            P("tensor", "dp", None),
            P("tensor", None),
            P("tensor", None),
            P("tensor", None),
            P("tensor", None),
            P(),
            P(),
        ),
        out_specs=(P("dp", "tensor"), P("tensor", None, None), P("tensor", None, None)),
        check_vma=False,
    )
```

```python
import jax
import jax.numpy as jnp
import numpy as np
from jax import lax
from jax.experimental import pallas as pl
from jax.experimental.pallas import tpu as pltpu
from jax.sharding import PartitionSpec as P

BLOCK = 64
HPD = 4
NX, NZ, NY = 4, 16, 4
BF = jnp.bfloat16
F32 = jnp.float32
VM = pl.BlockSpec(memory_space=pltpu.VMEM)
SM = pl.BlockSpec(memory_space=pltpu.SMEM)


def from_tensor(value, dx, dz):
    pairs = [
        (((x + dx) % NX) * NZ + (z + dz) % NZ, x * NZ + z) for x in range(NX) for z in range(NZ)
    ]
    return lax.ppermute(value, "tensor", pairs)


def from_core(value):
    return lax.ppermute(value, "dp", [(d ^ 1, d) for d in range(2 * NY)])


def add(*parts):
    total = parts[0].astype(F32)
    for part in parts[1:]:
        total = total + part.astype(F32)
    return total.astype(BF)


Z_ORDER = (0, 5, 11, 1, 6, 12, 15, 4, 10, 2, 7, 13, 14, 3, 9, 8)
Z_SLOT = np.argsort(np.array(Z_ORDER)).astype(np.int32)


def gather_features(tokens, grad_out):
    own = jnp.stack([tokens, grad_out])[:, None]
    plus, minus = from_tensor(own, 0, 5), from_tensor(own, 0, -5)
    three = jnp.concatenate([own, plus, minus], axis=1)
    parts = [three] + [from_tensor(three, 0, dz) for dz in (1, -1, 2, -2)] + [from_tensor(plus, 0, 3)]
    x, dy = (jnp.concatenate([part[i] for part in parts]) for i in range(2))
    x_plus, dy_minus = from_tensor(x, 1, 0), from_tensor(dy, -1, 0)
    dy_plus, x_minus = from_tensor(dy, 1, 0), from_tensor(x, -1, 0)
    x_two, dy_two = from_tensor(x_plus, 1, 0), from_tensor(dy_minus, -1, 0)
    return (x, x_plus, x_two, x_minus, dy, dy_plus, dy_two, dy_minus), (plus, minus)


def block_place(cols):
    me = lax.axis_index("tensor")
    owner = cols // 2
    dx = (owner // NZ - me // NZ) % NX
    dz = (owner - me) % NZ
    slot = jnp.sum(jnp.where(dz[:, None] == jnp.arange(NZ), Z_SLOT[None], 0), axis=1)
    return ((dx * NZ + slot) * 2 + cols % 2).astype(jnp.int32)


def left_half():
    return lax.broadcasted_iota(jnp.int32, (BLOCK, 2 * BLOCK), 1) < BLOCK


def swap_halves(tile):
    return jnp.concatenate([tile[:, BLOCK:], tile[:, :BLOCK]], axis=1)


def spread_kernel(up_at, up_loc, down_at, down_loc, pairs, up_dense, down_dense):
    left = left_half()

    def clear(i, _):
        up_dense[pl.ds(2 * i, 2)] = jnp.zeros((2, 256, 128), BF)
        down_dense[pl.ds(2 * i, 2)] = jnp.zeros((2, 256, 128), BF)
        return 0

    lax.fori_loop(0, 32, clear, 0)

    def place(g, _):
        for p in range(8):
            for which, at_ref, loc_ref, dense in (
                (0, up_at, up_loc, up_dense),
                (1, down_at, down_loc, down_dense),
            ):
                tile = pairs[g, which, p]
                turned = swap_halves(tile)
                for side in range(2):
                    slot = g * 16 + side * 8 + p
                    at, loc = at_ref[slot], loc_ref[slot]
                    half = at % 2
                    view = dense.at[at // 2, pl.ds(pl.multiple_of(loc * BLOCK, BLOCK), BLOCK), :]
                    value = jnp.where(half == side, tile, turned)
                    view[...] = jnp.where(left == (half == 0), value, view[...])
        return 0

    lax.fori_loop(0, 8, place, 0)


def spread_weights(tables, pairs):
    shape = jax.ShapeDtypeStruct((64, 256, 128), BF)
    return pl.pallas_call(
        spread_kernel,
        in_specs=[SM] * 4 + [VM],
        out_specs=[VM, VM],
        out_shape=[shape, shape],
        compiler_params=pltpu.CompilerParams(vmem_limit_bytes=16 << 20),
        cost_estimate=pl.CostEstimate(flops=0, bytes_accessed=12 << 20, transcendentals=0),
        name="spread_weights",
    )(*tables, pairs)


def exchange_order(outward):
    row = lax.broadcasted_iota(jnp.int32, (512, 512), 0 if outward else 1)
    col = lax.broadcasted_iota(jnp.int32, (512, 512), 1 if outward else 0)
    return ((row % 8) * BLOCK + row // 8 == col).astype(F32).astype(BF)


def wide(ref, start, count):
    return jnp.concatenate([ref[start + i] for i in range(count)], axis=1)


def times_dense(features, dense):
    total = None
    for part in range(4):
        for first in (0, 8):
            term = lax.dot_general(
                wide(features[part], first, 8),
                wide(dense, part * 16 + first, 8),
                (((1,), (1,)), ((), ())),
                preferred_element_type=F32,
            )
            total = term if total is None else total + term
    return total


def forward_kernel(*refs):
    xs, dys, (up_dense, down_dense, out, slope) = refs[:4], refs[4:8], refs[8:]
    pre = times_dense(xs, up_dense)
    cdf = 0.5 * (1.0 + lax.erf(pre * 0.7071067811865476))
    slope[...] = cdf + pre * jnp.exp(-0.5 * pre * pre) * 0.3989422804014327
    hidden = (pre * cdf).astype(BF)
    both = jnp.concatenate([hidden, times_dense(dys, down_dense).astype(BF)], axis=1)
    out[...] = lax.dot_general(
        exchange_order(True), both, (((1,), (1,)), ((), ())), preferred_element_type=F32
    ).astype(BF)


def forward(features, up_dense, down_dense):
    return pl.pallas_call(
        forward_kernel,
        in_specs=[VM] * 10,
        out_specs=[VM, VM],
        out_shape=[
            jax.ShapeDtypeStruct((512, 128), BF),
            jax.ShapeDtypeStruct((128, 256), F32),
        ],
        compiler_params=pltpu.CompilerParams(vmem_limit_bytes=28 << 20),
        cost_estimate=pl.CostEstimate(flops=1 << 30, bytes_accessed=12 << 20, transcendentals=1 << 16),
        name="forward",
    )(*features, up_dense, down_dense)


def input_kernel(z_slot, dpre_ref, up_w, near, to_plus, to_minus, later):
    dpre = dpre_ref[...]

    def terms(target, z, part):
        w = jnp.concatenate([up_w[part * NZ + z_slot[z + j]] for j in range(2)], axis=1)
        value = jnp.dot(dpre, w, preferred_element_type=F32).astype(BF)
        target[z] = value[:, :128]
        target[z + 1] = value[:, 128:]

    for z in range(0, NZ, 2):
        low = z < NZ // 2
        terms(to_plus, z, 2 if low else 1)
        terms(to_minus, z, 3 if low else 2)
        terms(later, z, 1 if low else 3)
        terms(near, z, 0)


def input_terms(z_slot, dpre, up_w):
    chunk = jax.ShapeDtypeStruct((NZ, 128, 128), BF)
    return pl.pallas_call(
        input_kernel,
        in_specs=[SM] + [VM] * 2,
        out_specs=[VM] * 4,
        out_shape=[chunk] * 4,
        compiler_params=pltpu.CompilerParams(vmem_limit_bytes=20 << 20),
        cost_estimate=pl.CostEstimate(flops=1 << 29, bytes_accessed=6 << 20, transcendentals=0),
        name="input_terms",
    )(z_slot, dpre, up_w)


def weight_kernel(up_at, up_loc, down_at, down_loc, *refs):
    xs, dys = refs[:4], refs[4:8]
    back, slope, out, dpre_out, up_dense, down_dense = refs[8:]
    left = left_half()
    scale = 1.0 / 32.0
    both = jnp.dot(exchange_order(False), back[...], preferred_element_type=F32)
    hidden_t = both[:256].astype(BF)
    dpre = both[256:].T * slope[...]
    dpre_out[...] = dpre.astype(BF)
    dpre_t = dpre.T.astype(BF)
    for part in range(4):

        def step(i, _, part=part):
            at = part * 16 + 2 * i
            for lhs, source, dense in ((dpre_t, xs, up_dense), (hidden_t, dys, down_dense)):
                value = jnp.dot(lhs, wide(source[part], 2 * i, 2), preferred_element_type=F32)
                value = (value * scale).astype(BF)
                dense[at] = value[:, :128]
                dense[at + 1] = value[:, 128:]
            return 0

        lax.fori_loop(0, 8, step, 0, unroll=2)

    def pick(device, _):
        for p in range(8):
            for which, at_ref, loc_ref, dense in (
                (0, up_at, up_loc, up_dense),
                (1, down_at, down_loc, down_dense),
            ):
                sides = []
                for side in range(2):
                    slot = device * 16 + side * 8 + p
                    at, loc = at_ref[slot], loc_ref[slot]
                    tile = dense[at // 2, pl.ds(pl.multiple_of(loc * BLOCK, BLOCK), BLOCK), :]
                    sides.append(jnp.where(at % 2 == side, tile, swap_halves(tile)))
                out[device, which, p] = jnp.where(left, sides[0], sides[1])
        return 0

    lax.fori_loop(0, 8, pick, 0)


def weight_terms(tables, features, back, slope):
    return pl.pallas_call(
        weight_kernel,
        in_specs=[SM] * 4 + [VM] * 10,
        out_specs=[VM, VM],
        out_shape=[
            jax.ShapeDtypeStruct((8, 2, 8, BLOCK, 128), BF),
            jax.ShapeDtypeStruct((128, 256), BF),
        ],
        scratch_shapes=[pltpu.VMEM((64, 256, 128), BF), pltpu.VMEM((64, 256, 128), BF)],
        compiler_params=pltpu.CompilerParams(vmem_limit_bytes=24 << 20),
        cost_estimate=pl.CostEstimate(flops=3 << 29, bytes_accessed=14 << 20, transcendentals=0),
        name="weight_terms",
    )(*tables, *features, back, slope)


def pack_kernel(up, down, out):
    for which, ref in ((0, up), (1, down)):
        rows = []
        for at in range(0, BLOCK * BLOCK, 2 * BLOCK):
            tile = ref[:, at : at + 2 * BLOCK].astype(F32)
            for side in (slice(0, BLOCK), slice(BLOCK, 2 * BLOCK)):
                rows.append(jnp.concatenate([tile[:8, side], tile[8:, side]], axis=1))
        pairs = jnp.swapaxes(jnp.stack(rows), 0, 1)
        for p in range(8):
            pair = pairs[p]
            if which == 0:
                pair = pair.T
                pair = jnp.concatenate([pair[:BLOCK], pair[BLOCK:]], axis=1)
            out[which, p] = pair.astype(BF)


def pack(up, down):
    return pl.pallas_call(
        pack_kernel,
        in_specs=[VM, VM],
        out_specs=VM,
        out_shape=jax.ShapeDtypeStruct((2, 8, BLOCK, 2 * BLOCK), BF),
        compiler_params=pltpu.CompilerParams(vmem_limit_bytes=8 << 20),
        cost_estimate=pl.CostEstimate(flops=0, bytes_accessed=1 << 19, transcendentals=0),
        name="pack",
    )(up, down)


def unpack(pairs, turned=False):
    axis = 1 if turned else 2
    slots = jnp.concatenate(jnp.split(pairs, 2, axis=axis))
    return slots.reshape(16, BLOCK * BLOCK)


Y_GROUPS = [[y * 2 + c for y in range(NY)] for c in range(2)]
Z_GROUPS = [[x * NZ + z for z in range(NZ)] for x in range(NX)]


def exchange(rows):
    return lax.all_to_all(rows.reshape(64, 8, 128), "tensor", 0, 0, tiled=True).reshape(512, 128)


def place_kernel(me_ref, mine, theirs, parts, up, down, tokens):
    tokens[...] = jnp.sum(parts[...].astype(F32), axis=0).astype(BF)
    core = me_ref[0] % 2
    for y in range(NY):
        for c in range(2):
            rows = pl.ds((y * 2 + c) * 16, 16)
            up[rows] = jnp.where(core == c, mine[y, 0], theirs[y, 0])
            down[rows] = jnp.where(core == c, mine[y, 1], theirs[y, 1])


def place_slots(me, mine, theirs, parts):
    shape = jax.ShapeDtypeStruct((128, BLOCK * BLOCK), BF)
    return pl.pallas_call(
        place_kernel,
        in_specs=[SM, VM, VM, VM],
        out_specs=[VM, VM, VM],
        out_shape=[shape, shape, jax.ShapeDtypeStruct((128, 128), BF)],
        compiler_params=pltpu.CompilerParams(vmem_limit_bytes=8 << 20),
        cost_estimate=pl.CostEstimate(flops=0, bytes_accessed=4 << 20, transcendentals=0),
        name="place_slots",
    )(me, mine, theirs, parts)


def reduce_all(me, slots, near, to_plus, to_minus, later):
    half = NZ // 2
    order = lax.optimization_barrier
    got_plus, got_minus = from_tensor(to_plus, -1, 0), from_tensor(to_minus, 1, 0)
    slots = lax.all_to_all(slots, "dp", 0, 0, tiled=True)
    on_plus, on_minus = add(later[:half], got_plus[:half]), add(later[half:], got_minus[half:])
    low, high = from_tensor(on_plus, -1, 0), from_tensor(on_minus, 1, 0)
    low = add(near[:half], low, got_minus[:half])
    high = add(near[half:], got_plus[half:], high)
    column = jnp.concatenate([low, high])
    slots, _ = order((slots, column))
    own = jnp.sum(slots.astype(F32), axis=0).astype(BF)
    own = jnp.stack([unpack(jnp.swapaxes(own[0], 1, 2), True), unpack(own[1])])
    column, own = order((column, own))
    parts = lax.all_to_all(column, "tensor", 0, 0, tiled=True, axis_index_groups=Z_GROUPS)
    mine = lax.all_gather(own, "dp", axis=0, axis_index_groups=Y_GROUPS)
    up, down, grad_tokens = place_slots(me, mine, from_core(mine), parts)
    return grad_tokens, up[None], down[None]


def per_device(
    tokens,
    grad_out,
    up_weight,
    down_weight,
    up_local,
    up_col,
    down_local,
    down_col,
    up_perm,
    down_perm,
):
    features, first = gather_features(tokens, grad_out)
    up_own, down_own, *_ = lax.optimization_barrier((up_weight[0], down_weight[0], *first))
    pairs = lax.all_gather(pack(up_own, down_own), "dp", axis=0)
    tables = (block_place(up_col[0]), up_local[0], block_place(down_col[0]), down_local[0])
    up4, down4 = up_perm.reshape(-1, HPD), down_perm.reshape(-1, HPD)
    wanted = jnp.stack([down4, up4 + 256], axis=1).reshape(-1)
    present = jnp.stack([up4, down4 + 256], axis=1).reshape(-1)
    route = (wanted[:, None] == present[None, :]).astype(BF)
    z_from_me = (jnp.arange(NZ) - lax.axis_index("tensor")) % NZ
    z_slot = jnp.sum(jnp.where(z_from_me[:, None] == jnp.arange(NZ), Z_SLOT[None], 0), axis=1)

    up_dense, down_dense = spread_weights(tables, pairs)
    sent, slope = forward(features, up_dense, down_dense)
    routed = jnp.dot(route, exchange(sent), preferred_element_type=F32).astype(BF)
    back = exchange(routed)
    me = lax.axis_index("dp").astype(jnp.int32).reshape(1)
    slots, dpre = weight_terms(tables, features, back, slope)
    return reduce_all(me, slots, *input_terms(z_slot.astype(jnp.int32), dpre, up_dense))


def solution(mesh):
    return jax.shard_map(
        per_device,
        mesh=mesh,
        in_specs=(
            P("dp", "tensor"),
            P("dp", "tensor"),
            P("tensor", "dp", None),
            P("tensor", "dp", None),
            P("tensor", None),
            P("tensor", None),
            P("tensor", None),
            P("tensor", None),
            P(),
            P(),
        ),
        out_specs=(P("dp", "tensor"), P("tensor", None, None), P("tensor", None, None)),
        check_vma=False,
    )
```

```python
import jax
import jax.numpy as jnp
import numpy as np
from jax import lax
from jax.experimental import pallas as pl
from jax.experimental.pallas import tpu as pltpu
from jax.sharding import PartitionSpec as P

BLOCK = 64
HPD = 4
NX, NZ, NY = 4, 16, 4
BF = jnp.bfloat16
F32 = jnp.float32
VM = pl.BlockSpec(memory_space=pltpu.VMEM)
SM = pl.BlockSpec(memory_space=pltpu.SMEM)


def from_tensor(value, dx, dz):
    pairs = [
        (((x + dx) % NX) * NZ + (z + dz) % NZ, x * NZ + z) for x in range(NX) for z in range(NZ)
    ]
    return lax.ppermute(value, "tensor", pairs)


def from_core(value):
    return lax.ppermute(value, "dp", [(d ^ 1, d) for d in range(2 * NY)])


def add(*parts):
    total = parts[0].astype(F32)
    for part in parts[1:]:
        total = total + part.astype(F32)
    return total.astype(BF)


Z_ORDER = (0, 5, 11, 1, 6, 12, 15, 4, 10, 2, 7, 13, 14, 3, 9, 8)
Z_SLOT = np.argsort(np.array(Z_ORDER)).astype(np.int32)


def gather_features(tokens, grad_out):
    own = jnp.stack([tokens, grad_out])[:, None]
    plus, minus = from_tensor(own, 0, 5), from_tensor(own, 0, -5)
    three = jnp.concatenate([own, plus, minus], axis=1)
    parts = [three] + [from_tensor(three, 0, dz) for dz in (1, -1, 2, -2)] + [from_tensor(plus, 0, 3)]
    x, dy = (jnp.concatenate([part[i] for part in parts]) for i in range(2))
    x_plus, dy_minus = from_tensor(x, 1, 0), from_tensor(dy, -1, 0)
    dy_plus, x_minus = from_tensor(dy, 1, 0), from_tensor(x, -1, 0)
    x_two, dy_two = from_tensor(x_plus, 1, 0), from_tensor(dy_minus, -1, 0)
    return (x, x_plus, x_two, x_minus, dy, dy_plus, dy_two, dy_minus), (plus, minus)


def block_place(cols):
    me = lax.axis_index("tensor")
    owner = cols // 2
    dx = (owner // NZ - me // NZ) % NX
    dz = (owner - me) % NZ
    slot = jnp.sum(jnp.where(dz[:, None] == jnp.arange(NZ), Z_SLOT[None], 0), axis=1)
    return ((dx * NZ + slot) * 2 + cols % 2).astype(jnp.int32)


def left_half():
    return lax.broadcasted_iota(jnp.int32, (BLOCK, 2 * BLOCK), 1) < BLOCK


def swap_halves(tile):
    return jnp.concatenate([tile[:, BLOCK:], tile[:, :BLOCK]], axis=1)


def spread_kernel(up_at, up_loc, down_at, down_loc, pairs, up_dense, down_dense):
    left = left_half()

    def clear(i, _):
        up_dense[pl.ds(2 * i, 2)] = jnp.zeros((2, 256, 128), BF)
        down_dense[pl.ds(2 * i, 2)] = jnp.zeros((2, 256, 128), BF)
        return 0

    lax.fori_loop(0, 32, clear, 0)

    def place(g, _):
        for p in range(8):
            for which, at_ref, loc_ref, dense in (
                (0, up_at, up_loc, up_dense),
                (1, down_at, down_loc, down_dense),
            ):
                tile = pairs[g, which, p]
                turned = swap_halves(tile)
                for side in range(2):
                    slot = g * 16 + side * 8 + p
                    at, loc = at_ref[slot], loc_ref[slot]
                    half = at % 2
                    view = dense.at[at // 2, pl.ds(pl.multiple_of(loc * BLOCK, BLOCK), BLOCK), :]
                    value = jnp.where(half == side, tile, turned)
                    view[...] = jnp.where(left == (half == 0), value, view[...])
        return 0

    lax.fori_loop(0, 8, place, 0)


def spread_weights(tables, pairs):
    shape = jax.ShapeDtypeStruct((64, 256, 128), BF)
    return pl.pallas_call(
        spread_kernel,
        in_specs=[SM] * 4 + [VM],
        out_specs=[VM, VM],
        out_shape=[shape, shape],
        compiler_params=pltpu.CompilerParams(vmem_limit_bytes=16 << 20),
        cost_estimate=pl.CostEstimate(flops=0, bytes_accessed=12 << 20, transcendentals=0),
        name="spread_weights",
    )(*tables, pairs)


def exchange_order(outward):
    row = lax.broadcasted_iota(jnp.int32, (512, 512), 0 if outward else 1)
    col = lax.broadcasted_iota(jnp.int32, (512, 512), 1 if outward else 0)
    return ((row % 8) * BLOCK + row // 8 == col).astype(F32).astype(BF)


def wide(ref, start, count):
    return jnp.concatenate([ref[start + i] for i in range(count)], axis=1)


def times_dense(features, dense):
    total = None
    for part in range(4):
        for first in (0, 8):
            term = lax.dot_general(
                wide(features[part], first, 8),
                wide(dense, part * 16 + first, 8),
                (((1,), (1,)), ((), ())),
                preferred_element_type=F32,
            )
            total = term if total is None else total + term
    return total


def forward_kernel(*refs):
    xs, dys, (up_dense, down_dense, out, slope) = refs[:4], refs[4:8], refs[8:]
    pre = times_dense(xs, up_dense)
    cdf = 0.5 * (1.0 + lax.erf(pre * 0.7071067811865476))
    slope[...] = cdf + pre * jnp.exp(-0.5 * pre * pre) * 0.3989422804014327
    hidden = (pre * cdf).astype(BF)
    both = jnp.concatenate([hidden, times_dense(dys, down_dense).astype(BF)], axis=1)
    out[...] = lax.dot_general(
        exchange_order(True), both, (((1,), (1,)), ((), ())), preferred_element_type=F32
    ).astype(BF)


def forward(features, up_dense, down_dense):
    return pl.pallas_call(
        forward_kernel,
        in_specs=[VM] * 10,
        out_specs=[VM, VM],
        out_shape=[
            jax.ShapeDtypeStruct((512, 128), BF),
            jax.ShapeDtypeStruct((128, 256), F32),
        ],
        compiler_params=pltpu.CompilerParams(vmem_limit_bytes=28 << 20),
        cost_estimate=pl.CostEstimate(flops=1 << 30, bytes_accessed=12 << 20, transcendentals=1 << 16),
        name="forward",
    )(*features, up_dense, down_dense)


def input_kernel(z_slot, dpre_ref, up_w, near, to_plus, to_minus, later):
    dpre = dpre_ref[...]

    def terms(target, z, part):
        w = jnp.concatenate([up_w[part * NZ + z_slot[z + j]] for j in range(2)], axis=1)
        value = jnp.dot(dpre, w, preferred_element_type=F32).astype(BF)
        target[z] = value[:, :128]
        target[z + 1] = value[:, 128:]

    for z in range(0, NZ, 2):
        low = z < NZ // 2
        terms(to_plus, z, 2 if low else 1)
        terms(to_minus, z, 3 if low else 2)
        terms(later, z, 1 if low else 3)
        terms(near, z, 0)


def input_terms(z_slot, dpre, up_w):
    chunk = jax.ShapeDtypeStruct((NZ, 128, 128), BF)
    return pl.pallas_call(
        input_kernel,
        in_specs=[SM] + [VM] * 2,
        out_specs=[VM] * 4,
        out_shape=[chunk] * 4,
        compiler_params=pltpu.CompilerParams(vmem_limit_bytes=20 << 20),
        cost_estimate=pl.CostEstimate(flops=1 << 29, bytes_accessed=6 << 20, transcendentals=0),
        name="input_terms",
    )(z_slot, dpre, up_w)


def weight_kernel(up_at, up_loc, down_at, down_loc, *refs):
    xs, dys = refs[:4], refs[4:8]
    back, slope, out, dpre_out, up_dense, down_dense = refs[8:]
    left = left_half()
    scale = 1.0 / 32.0
    both = jnp.dot(exchange_order(False), back[...], preferred_element_type=F32)
    hidden_t = both[:256].astype(BF)
    dpre = both[256:].T * slope[...]
    dpre_out[...] = dpre.astype(BF)
    dpre_t = dpre.T.astype(BF)
    for part in range(4):

        def step(i, _, part=part):
            at = part * 16 + 2 * i
            for lhs, source, dense in ((dpre_t, xs, up_dense), (hidden_t, dys, down_dense)):
                value = jnp.dot(lhs, wide(source[part], 2 * i, 2), preferred_element_type=F32)
                value = (value * scale).astype(BF)
                dense[at] = value[:, :128]
                dense[at + 1] = value[:, 128:]
            return 0

        lax.fori_loop(0, 8, step, 0, unroll=2)

    def pick(device, _):
        for p in range(8):
            for which, at_ref, loc_ref, dense in (
                (0, up_at, up_loc, up_dense),
                (1, down_at, down_loc, down_dense),
            ):
                sides = []
                for side in range(2):
                    slot = device * 16 + side * 8 + p
                    at, loc = at_ref[slot], loc_ref[slot]
                    tile = dense[at // 2, pl.ds(pl.multiple_of(loc * BLOCK, BLOCK), BLOCK), :]
                    sides.append(jnp.where(at % 2 == side, tile, swap_halves(tile)))
                out[device, which, p] = jnp.where(left, sides[0], sides[1])
        return 0

    lax.fori_loop(0, 8, pick, 0)


def weight_terms(tables, features, back, slope):
    return pl.pallas_call(
        weight_kernel,
        in_specs=[SM] * 4 + [VM] * 10,
        out_specs=[VM, VM],
        out_shape=[
            jax.ShapeDtypeStruct((8, 2, 8, BLOCK, 128), BF),
            jax.ShapeDtypeStruct((128, 256), BF),
        ],
        scratch_shapes=[pltpu.VMEM((64, 256, 128), BF), pltpu.VMEM((64, 256, 128), BF)],
        compiler_params=pltpu.CompilerParams(vmem_limit_bytes=18 << 20),
        cost_estimate=pl.CostEstimate(flops=3 << 29, bytes_accessed=14 << 20, transcendentals=0),
        name="weight_terms",
    )(*tables, *features, back, slope)


def pack_kernel(up, down, first, second, out):
    del first, second
    for which, ref in ((0, up), (1, down)):
        rows = []
        for at in range(0, BLOCK * BLOCK, 2 * BLOCK):
            tile = ref[:, at : at + 2 * BLOCK].astype(F32)
            for side in (slice(0, BLOCK), slice(BLOCK, 2 * BLOCK)):
                rows.append(jnp.concatenate([tile[:8, side], tile[8:, side]], axis=1))
        pairs = jnp.swapaxes(jnp.stack(rows), 0, 1)
        for p in range(8):
            pair = pairs[p]
            if which == 0:
                pair = pair.T
                pair = jnp.concatenate([pair[:BLOCK], pair[BLOCK:]], axis=1)
            out[which, p] = pair.astype(BF)


def pack(up, down, first, second):
    return pl.pallas_call(
        pack_kernel,
        in_specs=[VM, VM] + [pl.BlockSpec(memory_space=pl.ANY)] * 2,
        out_specs=VM,
        out_shape=jax.ShapeDtypeStruct((2, 8, BLOCK, 2 * BLOCK), BF),
        compiler_params=pltpu.CompilerParams(vmem_limit_bytes=8 << 20),
        cost_estimate=pl.CostEstimate(flops=0, bytes_accessed=1 << 19, transcendentals=0),
        name="pack",
    )(up, down, first, second)


def unpack(pairs, turned=False):
    axis = 1 if turned else 2
    slots = jnp.concatenate(jnp.split(pairs, 2, axis=axis))
    return slots.reshape(16, BLOCK * BLOCK)


Y_GROUPS = [[y * 2 + c for y in range(NY)] for c in range(2)]
Z_GROUPS = [[x * NZ + z for z in range(NZ)] for x in range(NX)]


def exchange(rows):
    return lax.all_to_all(rows.reshape(64, 8, 128), "tensor", 0, 0, tiled=True).reshape(512, 128)


def place_kernel(me_ref, mine, theirs, parts, up, down, tokens):
    tokens[...] = jnp.sum(parts[...].astype(F32), axis=0).astype(BF)
    core = me_ref[0] % 2
    for y in range(NY):
        for c in range(2):
            rows = pl.ds((y * 2 + c) * 16, 16)
            up[rows] = jnp.where(core == c, mine[y, 0], theirs[y, 0])
            down[rows] = jnp.where(core == c, mine[y, 1], theirs[y, 1])


def place_slots(me, mine, theirs, parts):
    shape = jax.ShapeDtypeStruct((128, BLOCK * BLOCK), BF)
    return pl.pallas_call(
        place_kernel,
        in_specs=[SM, VM, VM, VM],
        out_specs=[VM, VM, VM],
        out_shape=[shape, shape, jax.ShapeDtypeStruct((128, 128), BF)],
        compiler_params=pltpu.CompilerParams(vmem_limit_bytes=48 << 20),
        cost_estimate=pl.CostEstimate(flops=0, bytes_accessed=4 << 20, transcendentals=0),
        name="place_slots",
    )(me, mine, theirs, parts)


def reduce_all(me, slots, near, to_plus, to_minus, later):
    half = NZ // 2
    order = lax.optimization_barrier
    got_plus, got_minus = from_tensor(to_plus, -1, 0), from_tensor(to_minus, 1, 0)
    slots = lax.all_to_all(slots, "dp", 0, 0, tiled=True)
    on_plus, on_minus = add(later[:half], got_plus[:half]), add(later[half:], got_minus[half:])
    low, high = from_tensor(on_plus, -1, 0), from_tensor(on_minus, 1, 0)
    low = add(near[:half], low, got_minus[:half])
    high = add(near[half:], got_plus[half:], high)
    column = jnp.concatenate([low, high])
    slots, _ = order((slots, column))
    own = jnp.sum(slots.astype(F32), axis=0).astype(BF)
    own = jnp.stack([unpack(jnp.swapaxes(own[0], 1, 2), True), unpack(own[1])])
    column, own = order((column, own))
    parts = lax.all_to_all(column, "tensor", 0, 0, tiled=True, axis_index_groups=Z_GROUPS)
    mine = lax.all_gather(own, "dp", axis=0, axis_index_groups=Y_GROUPS)
    up, down, grad_tokens = place_slots(me, mine, from_core(mine), parts)
    return grad_tokens, up[None], down[None]


def per_device(
    tokens,
    grad_out,
    up_weight,
    down_weight,
    up_local,
    up_col,
    down_local,
    down_col,
    up_perm,
    down_perm,
):
    features, first = gather_features(tokens, grad_out)
    pairs = lax.all_gather(pack(up_weight[0], down_weight[0], *first), "dp", axis=0)
    tables = (block_place(up_col[0]), up_local[0], block_place(down_col[0]), down_local[0])
    up4, down4 = up_perm.reshape(-1, HPD), down_perm.reshape(-1, HPD)
    wanted = jnp.stack([down4, up4 + 256], axis=1).reshape(-1)
    present = jnp.stack([up4, down4 + 256], axis=1).reshape(-1)
    route = (wanted[:, None] == present[None, :]).astype(BF)
    z_from_me = (jnp.arange(NZ) - lax.axis_index("tensor")) % NZ
    z_slot = jnp.sum(jnp.where(z_from_me[:, None] == jnp.arange(NZ), Z_SLOT[None], 0), axis=1)

    up_dense, down_dense = spread_weights(tables, pairs)
    sent, slope = forward(features, up_dense, down_dense)
    routed = jnp.dot(route, exchange(sent), preferred_element_type=F32).astype(BF)
    back = exchange(routed)
    me = lax.axis_index("dp").astype(jnp.int32).reshape(1)
    slots, dpre = weight_terms(tables, features, back, slope)
    return reduce_all(me, slots, *input_terms(z_slot.astype(jnp.int32), dpre, up_dense))


def solution(mesh):
    return jax.shard_map(
        per_device,
        mesh=mesh,
        in_specs=(
            P("dp", "tensor"),
            P("dp", "tensor"),
            P("tensor", "dp", None),
            P("tensor", "dp", None),
            P("tensor", None),
            P("tensor", None),
            P("tensor", None),
            P("tensor", None),
            P(),
            P(),
        ),
        out_specs=(P("dp", "tensor"), P("tensor", None, None), P("tensor", None, None)),
        check_vma=False,
    )
```

```python
import jax
import jax.numpy as jnp
import numpy as np
from jax import lax
from jax.experimental import pallas as pl
from jax.experimental.pallas import tpu as pltpu
from jax.sharding import PartitionSpec as P

BLOCK = 64
HPD = 4
NX, NZ, NY = 4, 16, 4
BF = jnp.bfloat16
F32 = jnp.float32
VM = pl.BlockSpec(memory_space=pltpu.VMEM)
WHOLE = pl.BlockSpec()
SM = pl.BlockSpec(memory_space=pltpu.SMEM)


def from_tensor(value, dx, dz):
    pairs = [
        (((x + dx) % NX) * NZ + (z + dz) % NZ, x * NZ + z) for x in range(NX) for z in range(NZ)
    ]
    return lax.ppermute(value, "tensor", pairs)


def from_core(value):
    return lax.ppermute(value, "dp", [(d ^ 1, d) for d in range(2 * NY)])


def add(*parts):
    total = parts[0].astype(F32)
    for part in parts[1:]:
        total = total + part.astype(F32)
    return total.astype(BF)


Z_ORDER = (0, 5, 11, 1, 6, 12, 15, 4, 10, 2, 7, 13, 14, 3, 9, 8)
Z_SLOT = np.argsort(np.array(Z_ORDER)).astype(np.int32)


def gather_features(tokens, grad_out):
    own = jnp.stack([tokens, grad_out])[:, None]
    plus, minus = from_tensor(own, 0, 5), from_tensor(own, 0, -5)
    three = jnp.concatenate([own, plus, minus], axis=1)
    parts = [three] + [from_tensor(three, 0, dz) for dz in (1, -1, 2, -2)] + [from_tensor(plus, 0, 3)]
    x, dy = (jnp.concatenate([part[i] for part in parts]) for i in range(2))
    x_plus, dy_minus = from_tensor(x, 1, 0), from_tensor(dy, -1, 0)
    dy_plus, x_minus = from_tensor(dy, 1, 0), from_tensor(x, -1, 0)
    x_two, dy_two = from_tensor(x_plus, 1, 0), from_tensor(dy_minus, -1, 0)
    return (x, x_plus, x_two, x_minus, dy, dy_plus, dy_two, dy_minus), (plus, minus)


def block_place(cols):
    me = lax.axis_index("tensor")
    owner = cols // 2
    dx = (owner // NZ - me // NZ) % NX
    dz = (owner - me) % NZ
    slot = jnp.sum(jnp.where(dz[:, None] == jnp.arange(NZ), Z_SLOT[None], 0), axis=1)
    return ((dx * NZ + slot) * 2 + cols % 2).astype(jnp.int32)


def left_half():
    return lax.broadcasted_iota(jnp.int32, (BLOCK, 2 * BLOCK), 1) < BLOCK


def swap_halves(tile):
    return jnp.concatenate([tile[:, BLOCK:], tile[:, :BLOCK]], axis=1)


def spread_kernel(up_at, up_loc, down_at, down_loc, pairs, up_dense, down_dense):
    left = left_half()

    def clear(i, _):
        up_dense[pl.ds(2 * i, 2)] = jnp.zeros((2, 256, 128), BF)
        down_dense[pl.ds(2 * i, 2)] = jnp.zeros((2, 256, 128), BF)
        return 0

    lax.fori_loop(0, 32, clear, 0)

    def place(g, _):
        for p in range(8):
            for which, at_ref, loc_ref, dense in (
                (0, up_at, up_loc, up_dense),
                (1, down_at, down_loc, down_dense),
            ):
                tile = pairs[g, which, p]
                turned = swap_halves(tile)
                for side in range(2):
                    slot = g * 16 + side * 8 + p
                    at, loc = at_ref[slot], loc_ref[slot]
                    half = at % 2
                    view = dense.at[at // 2, pl.ds(pl.multiple_of(loc * BLOCK, BLOCK), BLOCK), :]
                    value = jnp.where(half == side, tile, turned)
                    view[...] = jnp.where(left == (half == 0), value, view[...])
        return 0

    lax.fori_loop(0, 8, place, 0)


def spread_weights(tables, pairs):
    shape = jax.ShapeDtypeStruct((64, 256, 128), BF)
    return pl.pallas_call(
        spread_kernel,
        in_specs=[SM] * 4 + [WHOLE],
        out_specs=[VM, VM],
        out_shape=[shape, shape],
        compiler_params=pltpu.CompilerParams(vmem_limit_bytes=16 << 20),
        cost_estimate=pl.CostEstimate(flops=0, bytes_accessed=12 << 20, transcendentals=0),
        name="spread_weights",
    )(*tables, pairs)


def exchange_order(outward):
    row = lax.broadcasted_iota(jnp.int32, (512, 512), 0 if outward else 1)
    col = lax.broadcasted_iota(jnp.int32, (512, 512), 1 if outward else 0)
    return ((row % 8) * BLOCK + row // 8 == col).astype(F32).astype(BF)


def wide(ref, start, count):
    return jnp.concatenate([ref[start + i] for i in range(count)], axis=1)


def times_dense(features, dense):
    total = None
    for part in range(4):
        for first in (0, 8):
            term = lax.dot_general(
                wide(features[part], first, 8),
                wide(dense, part * 16 + first, 8),
                (((1,), (1,)), ((), ())),
                preferred_element_type=F32,
            )
            total = term if total is None else total + term
    return total


def forward_kernel(*refs):
    xs, dys, (up_dense, down_dense, out, slope) = refs[:4], refs[4:8], refs[8:]
    pre = times_dense(xs, up_dense)
    cdf = 0.5 * (1.0 + lax.erf(pre * 0.7071067811865476))
    slope[...] = cdf + pre * jnp.exp(-0.5 * pre * pre) * 0.3989422804014327
    hidden = (pre * cdf).astype(BF)
    both = jnp.concatenate([hidden, times_dense(dys, down_dense).astype(BF)], axis=1)
    out[...] = lax.dot_general(
        exchange_order(True), both, (((1,), (1,)), ((), ())), preferred_element_type=F32
    ).astype(BF)


def forward(features, up_dense, down_dense):
    return pl.pallas_call(
        forward_kernel,
        in_specs=[VM] * 10,
        out_specs=[VM, VM],
        out_shape=[
            jax.ShapeDtypeStruct((512, 128), BF),
            jax.ShapeDtypeStruct((128, 256), F32),
        ],
        compiler_params=pltpu.CompilerParams(vmem_limit_bytes=28 << 20),
        cost_estimate=pl.CostEstimate(flops=1 << 30, bytes_accessed=12 << 20, transcendentals=1 << 16),
        name="forward",
    )(*features, up_dense, down_dense)


def input_kernel(z_slot, dpre_ref, up_w, near, to_plus, to_minus, later):
    dpre = dpre_ref[...]

    def terms(target, z, part):
        w = jnp.concatenate([up_w[part * NZ + z_slot[z + j]] for j in range(2)], axis=1)
        value = jnp.dot(dpre, w, preferred_element_type=F32).astype(BF)
        target[z] = value[:, :128]
        target[z + 1] = value[:, 128:]

    for z in range(0, NZ, 2):
        low = z < NZ // 2
        terms(to_plus, z, 2 if low else 1)
        terms(to_minus, z, 3 if low else 2)
        terms(later, z, 1 if low else 3)
        terms(near, z, 0)


def input_terms(z_slot, dpre, up_w):
    chunk = jax.ShapeDtypeStruct((NZ, 128, 128), BF)
    return pl.pallas_call(
        input_kernel,
        in_specs=[SM, VM, WHOLE],
        out_specs=[VM] * 4,
        out_shape=[chunk] * 4,
        compiler_params=pltpu.CompilerParams(vmem_limit_bytes=20 << 20),
        cost_estimate=pl.CostEstimate(flops=1 << 29, bytes_accessed=6 << 20, transcendentals=0),
        name="input_terms",
    )(z_slot, dpre, up_w)


def weight_kernel(up_at, up_loc, down_at, down_loc, *refs):
    xs, dys = refs[:4], refs[4:8]
    back, slope, out, dpre_out, up_dense, down_dense = refs[8:]
    left = left_half()
    scale = 1.0 / 32.0
    both = jnp.dot(exchange_order(False), back[...], preferred_element_type=F32)
    hidden_t = both[:256].astype(BF)
    dpre = both[256:].T * slope[...]
    dpre_out[...] = dpre.astype(BF)
    dpre_t = dpre.T.astype(BF)
    for part in range(4):

        def step(i, _, part=part):
            at = part * 16 + 2 * i
            for lhs, source, dense in ((dpre_t, xs, up_dense), (hidden_t, dys, down_dense)):
                value = jnp.dot(lhs, wide(source[part], 2 * i, 2), preferred_element_type=F32)
                value = (value * scale).astype(BF)
                dense[at] = value[:, :128]
                dense[at + 1] = value[:, 128:]
            return 0

        lax.fori_loop(0, 8, step, 0, unroll=2)

    def pick(device, _):
        for p in range(8):
            for which, at_ref, loc_ref, dense in (
                (0, up_at, up_loc, up_dense),
                (1, down_at, down_loc, down_dense),
            ):
                sides = []
                for side in range(2):
                    slot = device * 16 + side * 8 + p
                    at, loc = at_ref[slot], loc_ref[slot]
                    tile = dense[at // 2, pl.ds(pl.multiple_of(loc * BLOCK, BLOCK), BLOCK), :]
                    sides.append(jnp.where(at % 2 == side, tile, swap_halves(tile)))
                out[device, which, p] = jnp.where(left, sides[0], sides[1])
        return 0

    lax.fori_loop(0, 8, pick, 0)


def weight_terms(tables, features, back, slope):
    return pl.pallas_call(
        weight_kernel,
        in_specs=[SM] * 4 + [VM] * 10,
        out_specs=[VM, VM],
        out_shape=[
            jax.ShapeDtypeStruct((8, 2, 8, BLOCK, 128), BF),
            jax.ShapeDtypeStruct((128, 256), BF),
        ],
        scratch_shapes=[pltpu.VMEM((64, 256, 128), BF), pltpu.VMEM((64, 256, 128), BF)],
        compiler_params=pltpu.CompilerParams(vmem_limit_bytes=18 << 20),
        cost_estimate=pl.CostEstimate(flops=3 << 29, bytes_accessed=14 << 20, transcendentals=0),
        name="weight_terms",
    )(*tables, *features, back, slope)


def pack_kernel(up, down, first, second, out):
    del first, second
    for which, ref in ((0, up), (1, down)):
        rows = []
        for at in range(0, BLOCK * BLOCK, 2 * BLOCK):
            tile = ref[:, at : at + 2 * BLOCK].astype(F32)
            for side in (slice(0, BLOCK), slice(BLOCK, 2 * BLOCK)):
                rows.append(jnp.concatenate([tile[:8, side], tile[8:, side]], axis=1))
        pairs = jnp.swapaxes(jnp.stack(rows), 0, 1)
        for p in range(8):
            pair = pairs[p]
            if which == 0:
                pair = pair.T
                pair = jnp.concatenate([pair[:BLOCK], pair[BLOCK:]], axis=1)
            out[which, p] = pair.astype(BF)


def pack(up, down, first, second):
    return pl.pallas_call(
        pack_kernel,
        in_specs=[WHOLE, WHOLE] + [pl.BlockSpec(memory_space=pl.ANY)] * 2,
        out_specs=VM,
        out_shape=jax.ShapeDtypeStruct((2, 8, BLOCK, 2 * BLOCK), BF),
        compiler_params=pltpu.CompilerParams(vmem_limit_bytes=8 << 20),
        cost_estimate=pl.CostEstimate(flops=0, bytes_accessed=1 << 19, transcendentals=0),
        name="pack",
    )(up, down, first, second)


def unpack(pairs, turned=False):
    axis = 1 if turned else 2
    slots = jnp.concatenate(jnp.split(pairs, 2, axis=axis))
    return slots.reshape(16, BLOCK * BLOCK)


Y_GROUPS = [[y * 2 + c for y in range(NY)] for c in range(2)]
Z_GROUPS = [[x * NZ + z for z in range(NZ)] for x in range(NX)]


def exchange(rows):
    return lax.all_to_all(rows.reshape(64, 8, 128), "tensor", 0, 0, tiled=True).reshape(512, 128)


def place_kernel(me_ref, mine, theirs, parts, up, down, tokens):
    tokens[...] = jnp.sum(parts[...].astype(F32), axis=0).astype(BF)
    core = me_ref[0] % 2
    for y in range(NY):
        for c in range(2):
            rows = pl.ds((y * 2 + c) * 16, 16)
            up[rows] = jnp.where(core == c, mine[y, 0], theirs[y, 0])
            down[rows] = jnp.where(core == c, mine[y, 1], theirs[y, 1])


def place_slots(me, mine, theirs, parts):
    shape = jax.ShapeDtypeStruct((128, BLOCK * BLOCK), BF)
    return pl.pallas_call(
        place_kernel,
        in_specs=[SM, WHOLE, VM, VM],
        out_specs=[VM, VM, VM],
        out_shape=[shape, shape, jax.ShapeDtypeStruct((128, 128), BF)],
        compiler_params=pltpu.CompilerParams(vmem_limit_bytes=16 << 20),
        cost_estimate=pl.CostEstimate(flops=0, bytes_accessed=4 << 20, transcendentals=0),
        name="place_slots",
    )(me, mine, theirs, parts)


def reduce_all(me, slots, near, to_plus, to_minus, later):
    half = NZ // 2
    order = lax.optimization_barrier
    got_plus, got_minus = from_tensor(to_plus, -1, 0), from_tensor(to_minus, 1, 0)
    slots = lax.all_to_all(slots, "dp", 0, 0, tiled=True)
    on_plus, on_minus = add(later[:half], got_plus[:half]), add(later[half:], got_minus[half:])
    low, high = from_tensor(on_plus, -1, 0), from_tensor(on_minus, 1, 0)
    low = add(near[:half], low, got_minus[:half])
    high = add(near[half:], got_plus[half:], high)
    column = jnp.concatenate([low, high])
    slots, _ = order((slots, column))
    own = jnp.sum(slots.astype(F32), axis=0).astype(BF)
    own = jnp.stack([unpack(jnp.swapaxes(own[0], 1, 2), True), unpack(own[1])])
    column, own = order((column, own))
    parts = lax.all_to_all(column, "tensor", 0, 0, tiled=True, axis_index_groups=Z_GROUPS)
    mine = lax.all_gather(own, "dp", axis=0, axis_index_groups=Y_GROUPS)
    up, down, grad_tokens = place_slots(me, mine, from_core(mine), parts)
    return grad_tokens, up[None], down[None]


def per_device(
    tokens,
    grad_out,
    up_weight,
    down_weight,
    up_local,
    up_col,
    down_local,
    down_col,
    up_perm,
    down_perm,
):
    features, first = gather_features(tokens, grad_out)
    pairs = lax.all_gather(pack(up_weight[0], down_weight[0], *first), "dp", axis=0)
    tables = (block_place(up_col[0]), up_local[0], block_place(down_col[0]), down_local[0])
    up4, down4 = up_perm.reshape(-1, HPD), down_perm.reshape(-1, HPD)
    wanted = jnp.stack([down4, up4 + 256], axis=1).reshape(-1)
    present = jnp.stack([up4, down4 + 256], axis=1).reshape(-1)
    route = (wanted[:, None] == present[None, :]).astype(BF)
    z_from_me = (jnp.arange(NZ) - lax.axis_index("tensor")) % NZ
    z_slot = jnp.sum(jnp.where(z_from_me[:, None] == jnp.arange(NZ), Z_SLOT[None], 0), axis=1)

    up_dense, down_dense = spread_weights(tables, pairs)
    sent, slope = forward(features, up_dense, down_dense)
    routed = jnp.dot(route, exchange(sent), preferred_element_type=F32).astype(BF)
    back = exchange(routed)
    me = lax.axis_index("dp").astype(jnp.int32).reshape(1)
    slots, dpre = weight_terms(tables, features, back, slope)
    return reduce_all(me, slots, *input_terms(z_slot.astype(jnp.int32), dpre, up_dense))


def solution(mesh):
    return jax.shard_map(
        per_device,
        mesh=mesh,
        in_specs=(
            P("dp", "tensor"),
            P("dp", "tensor"),
            P("tensor", "dp", None),
            P("tensor", "dp", None),
            P("tensor", None),
            P("tensor", None),
            P("tensor", None),
            P("tensor", None),
            P(),
            P(),
        ),
        out_specs=(P("dp", "tensor"), P("tensor", None, None), P("tensor", None, None)),
        check_vma=False,
    )
```

```python
import jax
import jax.numpy as jnp
import numpy as np
from jax import lax
from jax.experimental import pallas as pl
from jax.experimental.pallas import tpu as pltpu
from jax.sharding import PartitionSpec as P

BLOCK = 64
HPD = 4
NX, NZ, NY = 4, 16, 4
BF = jnp.bfloat16
F32 = jnp.float32
VM = pl.BlockSpec(memory_space=pltpu.VMEM)
WHOLE = pl.BlockSpec()
SM = pl.BlockSpec(memory_space=pltpu.SMEM)


def from_tensor(value, dx, dz):
    pairs = [
        (((x + dx) % NX) * NZ + (z + dz) % NZ, x * NZ + z) for x in range(NX) for z in range(NZ)
    ]
    return lax.ppermute(value, "tensor", pairs)


def from_core(value):
    return lax.ppermute(value, "dp", [(d ^ 1, d) for d in range(2 * NY)])


def add(*parts):
    total = parts[0].astype(F32)
    for part in parts[1:]:
        total = total + part.astype(F32)
    return total.astype(BF)


Z_ORDER = (0, 5, 11, 1, 6, 12, 15, 4, 10, 2, 7, 13, 14, 3, 9, 8)
Z_SLOT = np.argsort(np.array(Z_ORDER)).astype(np.int32)


def gather_features(tokens, grad_out):
    own = jnp.stack([tokens, grad_out])[:, None]
    plus, minus = from_tensor(own, 0, 5), from_tensor(own, 0, -5)
    three = jnp.concatenate([own, plus, minus], axis=1)
    parts = [three] + [from_tensor(three, 0, dz) for dz in (1, -1, 2, -2)] + [from_tensor(plus, 0, 3)]
    x, dy = (jnp.concatenate([part[i] for part in parts]) for i in range(2))
    x_plus, dy_minus = from_tensor(x, 1, 0), from_tensor(dy, -1, 0)
    dy_plus, x_minus = from_tensor(dy, 1, 0), from_tensor(x, -1, 0)
    x_two, dy_two = from_tensor(x_plus, 1, 0), from_tensor(dy_minus, -1, 0)
    return (x, x_plus, x_two, x_minus, dy, dy_plus, dy_two, dy_minus), (plus, minus)


def block_place(cols):
    me = lax.axis_index("tensor")
    owner = cols // 2
    dx = (owner // NZ - me // NZ) % NX
    dz = (owner - me) % NZ
    slot = jnp.sum(jnp.where(dz[:, None] == jnp.arange(NZ), Z_SLOT[None], 0), axis=1)
    return ((dx * NZ + slot) * 2 + cols % 2).astype(jnp.int32)


def left_half():
    return lax.broadcasted_iota(jnp.int32, (BLOCK, 2 * BLOCK), 1) < BLOCK


def swap_halves(tile):
    return jnp.concatenate([tile[:, BLOCK:], tile[:, :BLOCK]], axis=1)


def spread_kernel(up_at, up_loc, down_at, down_loc, pairs, up_dense, down_dense):
    left = left_half()

    def clear(i, _):
        up_dense[pl.ds(2 * i, 2)] = jnp.zeros((2, 256, 128), BF)
        down_dense[pl.ds(2 * i, 2)] = jnp.zeros((2, 256, 128), BF)
        return 0

    lax.fori_loop(0, 32, clear, 0)

    def place(g, _):
        for p in range(8):
            for which, at_ref, loc_ref, dense in (
                (0, up_at, up_loc, up_dense),
                (1, down_at, down_loc, down_dense),
            ):
                tile = pairs[g, which, p]
                turned = swap_halves(tile)
                for side in range(2):
                    slot = g * 16 + side * 8 + p
                    at, loc = at_ref[slot], loc_ref[slot]
                    half = at % 2
                    view = dense.at[at // 2, pl.ds(pl.multiple_of(loc * BLOCK, BLOCK), BLOCK), :]
                    value = jnp.where(half == side, tile, turned)
                    view[...] = jnp.where(left == (half == 0), value, view[...])
        return 0

    lax.fori_loop(0, 8, place, 0)


def spread_weights(tables, pairs):
    shape = jax.ShapeDtypeStruct((64, 256, 128), BF)
    return pl.pallas_call(
        spread_kernel,
        in_specs=[SM] * 4 + [WHOLE],
        out_specs=[VM, VM],
        out_shape=[shape, shape],
        compiler_params=pltpu.CompilerParams(vmem_limit_bytes=16 << 20),
        cost_estimate=pl.CostEstimate(flops=0, bytes_accessed=12 << 20, transcendentals=0),
        name="spread_weights",
    )(*tables, pairs)


def exchange_order(outward):
    row = lax.broadcasted_iota(jnp.int32, (512, 512), 0 if outward else 1)
    col = lax.broadcasted_iota(jnp.int32, (512, 512), 1 if outward else 0)
    return ((row % 8) * BLOCK + row // 8 == col).astype(F32).astype(BF)


def wide(ref, start, count):
    return jnp.concatenate([ref[start + i] for i in range(count)], axis=1)


def times_dense(features, dense):
    total = None
    for part in range(4):
        for first in (0, 8):
            term = lax.dot_general(
                wide(features[part], first, 8),
                wide(dense, part * 16 + first, 8),
                (((1,), (1,)), ((), ())),
                preferred_element_type=F32,
            )
            total = term if total is None else total + term
    return total


def forward_kernel(*refs):
    xs, dys, (up_dense, down_dense, out, slope) = refs[:4], refs[4:8], refs[8:]
    pre = times_dense(xs, up_dense)
    cdf = 0.5 * (1.0 + lax.erf(pre * 0.7071067811865476))
    slope[...] = cdf + pre * jnp.exp(-0.5 * pre * pre) * 0.3989422804014327
    hidden = (pre * cdf).astype(BF)
    both = jnp.concatenate([hidden, times_dense(dys, down_dense).astype(BF)], axis=1)
    out[...] = lax.dot_general(
        exchange_order(True), both, (((1,), (1,)), ((), ())), preferred_element_type=F32
    ).astype(BF)


def forward(features, up_dense, down_dense):
    return pl.pallas_call(
        forward_kernel,
        in_specs=[VM] * 10,
        out_specs=[VM, VM],
        out_shape=[
            jax.ShapeDtypeStruct((512, 128), BF),
            jax.ShapeDtypeStruct((128, 256), F32),
        ],
        compiler_params=pltpu.CompilerParams(vmem_limit_bytes=28 << 20),
        cost_estimate=pl.CostEstimate(flops=1 << 30, bytes_accessed=12 << 20, transcendentals=1 << 16),
        name="forward",
    )(*features, up_dense, down_dense)


def input_kernel(z_slot, dpre_ref, up_w, near, to_plus, to_minus, later):
    dpre = dpre_ref[...]

    def terms(target, z, part):
        w = jnp.concatenate([up_w[part * NZ + z_slot[z + j]] for j in range(2)], axis=1)
        value = jnp.dot(dpre, w, preferred_element_type=F32).astype(BF)
        target[z] = value[:, :128]
        target[z + 1] = value[:, 128:]

    for z in range(0, NZ, 2):
        low = z < NZ // 2
        terms(to_plus, z, 2 if low else 1)
        terms(to_minus, z, 3 if low else 2)
        terms(later, z, 1 if low else 3)
        terms(near, z, 0)


def input_terms(z_slot, dpre, up_w):
    chunk = jax.ShapeDtypeStruct((NZ, 128, 128), BF)
    return pl.pallas_call(
        input_kernel,
        in_specs=[SM, VM, WHOLE],
        out_specs=[VM] * 4,
        out_shape=[chunk] * 4,
        compiler_params=pltpu.CompilerParams(vmem_limit_bytes=20 << 20),
        cost_estimate=pl.CostEstimate(flops=1 << 29, bytes_accessed=6 << 20, transcendentals=0),
        name="input_terms",
    )(z_slot, dpre, up_w)


def weight_kernel(up_at, up_loc, down_at, down_loc, *refs):
    xs, dys = refs[:4], refs[4:8]
    back, slope, out, dpre_out, up_dense, down_dense = refs[8:]
    left = left_half()
    scale = 1.0 / 32.0
    both = jnp.dot(exchange_order(False), back[...], preferred_element_type=F32)
    hidden_t = both[:256].astype(BF)
    dpre = both[256:].T * slope[...]
    dpre_out[...] = dpre.astype(BF)
    dpre_t = dpre.T.astype(BF)
    for part in range(4):

        def step(i, _, part=part):
            at = part * 16 + 2 * i
            for lhs, source, dense in ((dpre_t, xs, up_dense), (hidden_t, dys, down_dense)):
                value = jnp.dot(lhs, wide(source[part], 2 * i, 2), preferred_element_type=F32)
                value = (value * scale).astype(BF)
                dense[at] = value[:, :128]
                dense[at + 1] = value[:, 128:]
            return 0

        lax.fori_loop(0, 8, step, 0, unroll=2)

    def pick(device, _):
        for p in range(8):
            for which, at_ref, loc_ref, dense in (
                (0, up_at, up_loc, up_dense),
                (1, down_at, down_loc, down_dense),
            ):
                sides = []
                for side in range(2):
                    slot = device * 16 + side * 8 + p
                    at, loc = at_ref[slot], loc_ref[slot]
                    tile = dense[at // 2, pl.ds(pl.multiple_of(loc * BLOCK, BLOCK), BLOCK), :]
                    sides.append(jnp.where(at % 2 == side, tile, swap_halves(tile)))
                out[device, which, p] = jnp.where(left, sides[0], sides[1])
        return 0

    lax.fori_loop(0, 8, pick, 0)


def weight_terms(tables, features, back, slope):
    return pl.pallas_call(
        weight_kernel,
        in_specs=[SM] * 4 + [VM] * 10,
        out_specs=[VM, VM],
        out_shape=[
            jax.ShapeDtypeStruct((8, 2, 8, BLOCK, 128), BF),
            jax.ShapeDtypeStruct((128, 256), BF),
        ],
        scratch_shapes=[pltpu.VMEM((64, 256, 128), BF), pltpu.VMEM((64, 256, 128), BF)],
        compiler_params=pltpu.CompilerParams(vmem_limit_bytes=18 << 20),
        cost_estimate=pl.CostEstimate(flops=3 << 29, bytes_accessed=14 << 20, transcendentals=0),
        name="weight_terms",
    )(*tables, *features, back, slope)


def pack_kernel(up, down, first, second, out):
    del first, second
    for which, ref in ((0, up), (1, down)):
        rows = []
        for at in range(0, BLOCK * BLOCK, 2 * BLOCK):
            tile = ref[:, at : at + 2 * BLOCK].astype(F32)
            for side in (slice(0, BLOCK), slice(BLOCK, 2 * BLOCK)):
                rows.append(jnp.concatenate([tile[:8, side], tile[8:, side]], axis=1))
        pairs = jnp.swapaxes(jnp.stack(rows), 0, 1)
        for p in range(8):
            pair = pairs[p]
            if which == 0:
                pair = pair.T
                pair = jnp.concatenate([pair[:BLOCK], pair[BLOCK:]], axis=1)
            out[which, p] = pair.astype(BF)


def pack(up, down, first, second):
    return pl.pallas_call(
        pack_kernel,
        in_specs=[WHOLE, WHOLE] + [pl.BlockSpec(memory_space=pl.ANY)] * 2,
        out_specs=VM,
        out_shape=jax.ShapeDtypeStruct((2, 8, BLOCK, 2 * BLOCK), BF),
        compiler_params=pltpu.CompilerParams(vmem_limit_bytes=8 << 20),
        cost_estimate=pl.CostEstimate(flops=0, bytes_accessed=1 << 19, transcendentals=0),
        name="pack",
    )(up, down, first, second)


def unpack(pairs, turned=False):
    axis = 1 if turned else 2
    slots = jnp.concatenate(jnp.split(pairs, 2, axis=axis))
    return slots.reshape(16, BLOCK * BLOCK)


Y_GROUPS = [[y * 2 + c for y in range(NY)] for c in range(2)]
Z_GROUPS = [[x * NZ + z for z in range(NZ)] for x in range(NX)]


def exchange(rows):
    return lax.all_to_all(rows.reshape(64, 8, 128), "tensor", 0, 0, tiled=True).reshape(512, 128)


def place_kernel(me_ref, mine, theirs, parts, up, down, tokens):
    tokens[...] = jnp.sum(parts[...].astype(F32), axis=0).astype(BF)
    core = me_ref[0] % 2
    for y in range(NY):
        for c in range(2):
            rows = pl.ds((y * 2 + c) * 16, 16)
            up[rows] = jnp.where(core == c, mine[y, 0], theirs[y, 0])
            down[rows] = jnp.where(core == c, mine[y, 1], theirs[y, 1])


def place_slots(me, mine, theirs, parts):
    shape = jax.ShapeDtypeStruct((128, BLOCK * BLOCK), BF)
    return pl.pallas_call(
        place_kernel,
        in_specs=[SM, WHOLE, VM, VM],
        out_specs=[VM, VM, VM],
        out_shape=[shape, shape, jax.ShapeDtypeStruct((128, 128), BF)],
        compiler_params=pltpu.CompilerParams(vmem_limit_bytes=16 << 20),
        cost_estimate=pl.CostEstimate(flops=0, bytes_accessed=4 << 20, transcendentals=0),
        name="place_slots",
    )(me, mine, theirs, parts)


def reduce_all(me, slots, near, to_plus, to_minus, later):
    half = NZ // 2
    order = lax.optimization_barrier
    got_plus, got_minus = from_tensor(to_plus, -1, 0), from_tensor(to_minus, 1, 0)
    slots = lax.all_to_all(slots, "dp", 0, 0, tiled=True)
    on_plus, on_minus = add(later[:half], got_plus[:half]), add(later[half:], got_minus[half:])
    low, high = from_tensor(on_plus, -1, 0), from_tensor(on_minus, 1, 0)
    low = add(near[:half], low, got_minus[:half])
    high = add(near[half:], got_plus[half:], high)
    column = jnp.concatenate([low, high])
    slots, *_ = order((slots, on_plus, on_minus))
    own = jnp.sum(slots.astype(F32), axis=0).astype(BF)
    own = jnp.stack([unpack(jnp.swapaxes(own[0], 1, 2), True), unpack(own[1])])
    column, own = order((column, own))
    parts = lax.all_to_all(column, "tensor", 0, 0, tiled=True, axis_index_groups=Z_GROUPS)
    mine = lax.all_gather(own, "dp", axis=0, axis_index_groups=Y_GROUPS)
    up, down, grad_tokens = place_slots(me, mine, from_core(mine), parts)
    return grad_tokens, up[None], down[None]


def per_device(
    tokens,
    grad_out,
    up_weight,
    down_weight,
    up_local,
    up_col,
    down_local,
    down_col,
    up_perm,
    down_perm,
):
    features, first = gather_features(tokens, grad_out)
    pairs = lax.all_gather(pack(up_weight[0], down_weight[0], *first), "dp", axis=0)
    tables = (block_place(up_col[0]), up_local[0], block_place(down_col[0]), down_local[0])
    up4, down4 = up_perm.reshape(-1, HPD), down_perm.reshape(-1, HPD)
    wanted = jnp.stack([down4, up4 + 256], axis=1).reshape(-1)
    present = jnp.stack([up4, down4 + 256], axis=1).reshape(-1)
    route = (wanted[:, None] == present[None, :]).astype(BF)
    z_from_me = (jnp.arange(NZ) - lax.axis_index("tensor")) % NZ
    z_slot = jnp.sum(jnp.where(z_from_me[:, None] == jnp.arange(NZ), Z_SLOT[None], 0), axis=1)

    up_dense, down_dense = spread_weights(tables, pairs)
    sent, slope = forward(features, up_dense, down_dense)
    routed = jnp.dot(route, exchange(sent), preferred_element_type=F32).astype(BF)
    back = exchange(routed)
    me = lax.axis_index("dp").astype(jnp.int32).reshape(1)
    slots, dpre = weight_terms(tables, features, back, slope)
    return reduce_all(me, slots, *input_terms(z_slot.astype(jnp.int32), dpre, up_dense))


def solution(mesh):
    return jax.shard_map(
        per_device,
        mesh=mesh,
        in_specs=(
            P("dp", "tensor"),
            P("dp", "tensor"),
            P("tensor", "dp", None),
            P("tensor", "dp", None),
            P("tensor", None),
            P("tensor", None),
            P("tensor", None),
            P("tensor", None),
            P(),
            P(),
        ),
        out_specs=(P("dp", "tensor"), P("tensor", None, None), P("tensor", None, None)),
        check_vma=False,
    )
```

```python
import jax
import jax.numpy as jnp
import numpy as np
from jax import lax
from jax.experimental import pallas as pl
from jax.experimental.pallas import tpu as pltpu
from jax.sharding import PartitionSpec as P

BLOCK = 64
HPD = 4
NX, NZ, NY = 4, 16, 4
BF = jnp.bfloat16
F32 = jnp.float32
VM = pl.BlockSpec(memory_space=pltpu.VMEM)
WHOLE = pl.BlockSpec()
SM = pl.BlockSpec(memory_space=pltpu.SMEM)


def from_tensor(value, dx, dz):
    pairs = [
        (((x + dx) % NX) * NZ + (z + dz) % NZ, x * NZ + z) for x in range(NX) for z in range(NZ)
    ]
    return lax.ppermute(value, "tensor", pairs)


def from_core(value):
    return lax.ppermute(value, "dp", [(d ^ 1, d) for d in range(2 * NY)])


def add(*parts):
    total = parts[0].astype(F32)
    for part in parts[1:]:
        total = total + part.astype(F32)
    return total.astype(BF)


Z_ORDER = (0, 5, 11, 1, 6, 12, 15, 4, 10, 2, 7, 13, 14, 3, 9, 8)
Z_SLOT = np.argsort(np.array(Z_ORDER)).astype(np.int32)


def gather_features(tokens, grad_out):
    own = jnp.stack([tokens, grad_out])[:, None]
    plus, minus = from_tensor(own, 0, 5), from_tensor(own, 0, -5)
    three = jnp.concatenate([own, plus, minus], axis=1)
    parts = [three] + [from_tensor(three, 0, dz) for dz in (1, -1, 2, -2)] + [from_tensor(plus, 0, 3)]
    x, dy = (jnp.concatenate([part[i] for part in parts]) for i in range(2))
    x_plus, dy_minus = from_tensor(x, 1, 0), from_tensor(dy, -1, 0)
    dy_plus, x_minus = from_tensor(dy, 1, 0), from_tensor(x, -1, 0)
    x_two, dy_two = from_tensor(x_plus, 1, 0), from_tensor(dy_minus, -1, 0)
    return (x, x_plus, x_two, x_minus, dy, dy_plus, dy_two, dy_minus), (plus, minus)


def block_place(cols):
    me = lax.axis_index("tensor")
    owner = cols // 2
    dx = (owner // NZ - me // NZ) % NX
    dz = (owner - me) % NZ
    slot = jnp.sum(jnp.where(dz[:, None] == jnp.arange(NZ), Z_SLOT[None], 0), axis=1)
    return ((dx * NZ + slot) * 2 + cols % 2).astype(jnp.int32)


def left_half():
    return lax.broadcasted_iota(jnp.int32, (BLOCK, 2 * BLOCK), 1) < BLOCK


def swap_halves(tile):
    return jnp.concatenate([tile[:, BLOCK:], tile[:, :BLOCK]], axis=1)


def spread_kernel(up_at, up_loc, down_at, down_loc, pairs, up_dense, down_dense):
    left = left_half()

    def clear(i, _):
        up_dense[pl.ds(2 * i, 2)] = jnp.zeros((2, 256, 128), BF)
        down_dense[pl.ds(2 * i, 2)] = jnp.zeros((2, 256, 128), BF)
        return 0

    lax.fori_loop(0, 32, clear, 0)

    def place(g, _):
        for p in range(8):
            for which, at_ref, loc_ref, dense in (
                (0, up_at, up_loc, up_dense),
                (1, down_at, down_loc, down_dense),
            ):
                tile = pairs[g, which, p]
                turned = swap_halves(tile)
                for side in range(2):
                    slot = g * 16 + side * 8 + p
                    at, loc = at_ref[slot], loc_ref[slot]
                    half = at % 2
                    view = dense.at[at // 2, pl.ds(pl.multiple_of(loc * BLOCK, BLOCK), BLOCK), :]
                    value = jnp.where(half == side, tile, turned)
                    view[...] = jnp.where(left == (half == 0), value, view[...])
        return 0

    lax.fori_loop(0, 8, place, 0)


def spread_weights(tables, pairs):
    shape = jax.ShapeDtypeStruct((64, 256, 128), BF)
    return pl.pallas_call(
        spread_kernel,
        in_specs=[SM] * 4 + [WHOLE],
        out_specs=[VM, VM],
        out_shape=[shape, shape],
        compiler_params=pltpu.CompilerParams(vmem_limit_bytes=16 << 20),
        cost_estimate=pl.CostEstimate(flops=0, bytes_accessed=12 << 20, transcendentals=0),
        name="spread_weights",
    )(*tables, pairs)


def exchange_order(outward):
    row = lax.broadcasted_iota(jnp.int32, (512, 512), 0 if outward else 1)
    col = lax.broadcasted_iota(jnp.int32, (512, 512), 1 if outward else 0)
    return ((row % 8) * BLOCK + row // 8 == col).astype(F32).astype(BF)


def wide(ref, start, count):
    return jnp.concatenate([ref[start + i] for i in range(count)], axis=1)


def times_dense(features, dense):
    total = None
    for part in range(4):
        for first in (0, 8):
            term = lax.dot_general(
                wide(features[part], first, 8),
                wide(dense, part * 16 + first, 8),
                (((1,), (1,)), ((), ())),
                preferred_element_type=F32,
            )
            total = term if total is None else total + term
    return total


def forward_kernel(*refs):
    xs, dys, (up_dense, down_dense, out, slope) = refs[:4], refs[4:8], refs[8:]
    pre = times_dense(xs, up_dense)
    cdf = 0.5 * (1.0 + lax.erf(pre * 0.7071067811865476))
    slope[...] = cdf + pre * jnp.exp(-0.5 * pre * pre) * 0.3989422804014327
    hidden = (pre * cdf).astype(BF)
    both = jnp.concatenate([hidden, times_dense(dys, down_dense).astype(BF)], axis=1)
    out[...] = lax.dot_general(
        exchange_order(True), both, (((1,), (1,)), ((), ())), preferred_element_type=F32
    ).astype(BF)


def forward(features, up_dense, down_dense):
    return pl.pallas_call(
        forward_kernel,
        in_specs=[VM] * 10,
        out_specs=[VM, VM],
        out_shape=[
            jax.ShapeDtypeStruct((512, 128), BF),
            jax.ShapeDtypeStruct((128, 256), F32),
        ],
        compiler_params=pltpu.CompilerParams(vmem_limit_bytes=28 << 20),
        cost_estimate=pl.CostEstimate(flops=1 << 30, bytes_accessed=12 << 20, transcendentals=1 << 16),
        name="forward",
    )(*features, up_dense, down_dense)


def input_kernel(z_slot, dpre_ref, up_w, near, to_plus, to_minus, later):
    dpre = dpre_ref[...]

    def terms(target, z, part):
        w = jnp.concatenate([up_w[part * NZ + z_slot[z + j]] for j in range(2)], axis=1)
        value = jnp.dot(dpre, w, preferred_element_type=F32).astype(BF)
        target[z] = value[:, :128]
        target[z + 1] = value[:, 128:]

    for z in range(0, NZ, 2):
        low = z < NZ // 2
        terms(to_plus, z, 2 if low else 1)
        terms(to_minus, z, 3 if low else 2)
        terms(later, z, 1 if low else 3)
        terms(near, z, 0)


def input_terms(z_slot, dpre, up_w):
    chunk = jax.ShapeDtypeStruct((NZ, 128, 128), BF)
    return pl.pallas_call(
        input_kernel,
        in_specs=[SM, VM, WHOLE],
        out_specs=[VM] * 4,
        out_shape=[chunk] * 4,
        compiler_params=pltpu.CompilerParams(vmem_limit_bytes=20 << 20),
        cost_estimate=pl.CostEstimate(flops=1 << 29, bytes_accessed=6 << 20, transcendentals=0),
        name="input_terms",
    )(z_slot, dpre, up_w)


def weight_kernel(up_at, up_loc, down_at, down_loc, *refs):
    xs, dys = refs[:4], refs[4:8]
    back, slope, out, dpre_out, up_dense, down_dense = refs[8:]
    left = left_half()
    scale = 1.0 / 32.0
    both = jnp.dot(exchange_order(False), back[...], preferred_element_type=F32)
    hidden_t = both[:256].astype(BF)
    dpre = both[256:].T * slope[...]
    dpre_out[...] = dpre.astype(BF)
    dpre_t = dpre.T.astype(BF)
    for part in range(4):

        def step(i, _, part=part):
            at = part * 16 + 2 * i
            for lhs, source, dense in ((dpre_t, xs, up_dense), (hidden_t, dys, down_dense)):
                value = jnp.dot(lhs, wide(source[part], 2 * i, 2), preferred_element_type=F32)
                value = (value * scale).astype(BF)
                dense[at] = value[:, :128]
                dense[at + 1] = value[:, 128:]
            return 0

        lax.fori_loop(0, 8, step, 0, unroll=2)

    def pick(device, _):
        for p in range(8):
            for which, at_ref, loc_ref, dense in (
                (0, up_at, up_loc, up_dense),
                (1, down_at, down_loc, down_dense),
            ):
                sides = []
                for side in range(2):
                    slot = device * 16 + side * 8 + p
                    at, loc = at_ref[slot], loc_ref[slot]
                    tile = dense[at // 2, pl.ds(pl.multiple_of(loc * BLOCK, BLOCK), BLOCK), :]
                    sides.append(jnp.where(at % 2 == side, tile, swap_halves(tile)))
                out[device, which, p] = jnp.where(left, sides[0], sides[1])
        return 0

    lax.fori_loop(0, 8, pick, 0)


def weight_terms(tables, features, back, slope):
    return pl.pallas_call(
        weight_kernel,
        in_specs=[SM] * 4 + [VM] * 10,
        out_specs=[VM, VM],
        out_shape=[
            jax.ShapeDtypeStruct((8, 2, 8, BLOCK, 128), BF),
            jax.ShapeDtypeStruct((128, 256), BF),
        ],
        scratch_shapes=[pltpu.VMEM((64, 256, 128), BF), pltpu.VMEM((64, 256, 128), BF)],
        compiler_params=pltpu.CompilerParams(vmem_limit_bytes=18 << 20),
        cost_estimate=pl.CostEstimate(flops=3 << 29, bytes_accessed=14 << 20, transcendentals=0),
        name="weight_terms",
    )(*tables, *features, back, slope)


def pack_kernel(up, down, first, second, out):
    del first, second
    for which, ref in ((0, up), (1, down)):
        rows = []
        for at in range(0, BLOCK * BLOCK, 2 * BLOCK):
            tile = ref[:, at : at + 2 * BLOCK].astype(F32)
            for side in (slice(0, BLOCK), slice(BLOCK, 2 * BLOCK)):
                rows.append(jnp.concatenate([tile[:8, side], tile[8:, side]], axis=1))
        pairs = jnp.swapaxes(jnp.stack(rows), 0, 1)
        for p in range(8):
            pair = pairs[p]
            if which == 0:
                pair = pair.T
                pair = jnp.concatenate([pair[:BLOCK], pair[BLOCK:]], axis=1)
            out[which, p] = pair.astype(BF)


def pack(up, down, first, second):
    return pl.pallas_call(
        pack_kernel,
        in_specs=[WHOLE, WHOLE] + [pl.BlockSpec(memory_space=pl.ANY)] * 2,
        out_specs=VM,
        out_shape=jax.ShapeDtypeStruct((2, 8, BLOCK, 2 * BLOCK), BF),
        compiler_params=pltpu.CompilerParams(vmem_limit_bytes=8 << 20),
        cost_estimate=pl.CostEstimate(flops=0, bytes_accessed=1 << 19, transcendentals=0),
        name="pack",
    )(up, down, first, second)


def unpack(pairs, turned=False):
    axis = 1 if turned else 2
    slots = jnp.concatenate(jnp.split(pairs, 2, axis=axis))
    return slots.reshape(16, BLOCK * BLOCK)


Y_GROUPS = [[y * 2 + c for y in range(NY)] for c in range(2)]
Z_GROUPS = [[x * NZ + z for z in range(NZ)] for x in range(NX)]


def exchange(rows):
    return lax.all_to_all(rows.reshape(64, 8, 128), "tensor", 0, 0, tiled=True).reshape(512, 128)


def place_kernel(me_ref, mine, theirs, parts, up, down, tokens):
    tokens[...] = jnp.sum(parts[...].astype(F32), axis=0).astype(BF)
    core = me_ref[0] % 2
    for y in range(NY):
        for c in range(2):
            rows = pl.ds((y * 2 + c) * 16, 16)
            up[rows] = jnp.where(core == c, mine[y, 0], theirs[y, 0])
            down[rows] = jnp.where(core == c, mine[y, 1], theirs[y, 1])


def place_slots(me, mine, theirs, parts):
    shape = jax.ShapeDtypeStruct((128, BLOCK * BLOCK), BF)
    return pl.pallas_call(
        place_kernel,
        in_specs=[SM, WHOLE, VM, VM],
        out_specs=[VM, VM, VM],
        out_shape=[shape, shape, jax.ShapeDtypeStruct((128, 128), BF)],
        compiler_params=pltpu.CompilerParams(vmem_limit_bytes=16 << 20),
        cost_estimate=pl.CostEstimate(flops=0, bytes_accessed=4 << 20, transcendentals=0),
        name="place_slots",
    )(me, mine, theirs, parts)


def reduce_all(me, slots, near, to_plus, to_minus, later):
    half = NZ // 2
    order = lax.optimization_barrier
    got_plus, got_minus = from_tensor(to_plus, -1, 0), from_tensor(to_minus, 1, 0)
    slots = lax.all_to_all(slots, "dp", 0, 0, tiled=True)
    on_plus, on_minus = add(later[:half], got_plus[:half]), add(later[half:], got_minus[half:])
    low, high = from_tensor(on_plus, -1, 0), from_tensor(on_minus, 1, 0)
    slots, *_ = order((slots, on_plus, on_minus))
    own = jnp.sum(slots.astype(F32), axis=0).astype(BF)
    own = jnp.stack([unpack(jnp.swapaxes(own[0], 1, 2), True), unpack(own[1])])
    low, high, own = order((low, high, own))
    low = add(near[:half], low, got_minus[:half])
    high = add(near[half:], got_plus[half:], high)
    column = jnp.concatenate([low, high])
    column, own = order((column, own))
    parts = lax.all_to_all(column, "tensor", 0, 0, tiled=True, axis_index_groups=Z_GROUPS)
    mine = lax.all_gather(own, "dp", axis=0, axis_index_groups=Y_GROUPS)
    up, down, grad_tokens = place_slots(me, mine, from_core(mine), parts)
    return grad_tokens, up[None], down[None]


def per_device(
    tokens,
    grad_out,
    up_weight,
    down_weight,
    up_local,
    up_col,
    down_local,
    down_col,
    up_perm,
    down_perm,
):
    features, first = gather_features(tokens, grad_out)
    pairs = lax.all_gather(pack(up_weight[0], down_weight[0], *first), "dp", axis=0)
    tables = (block_place(up_col[0]), up_local[0], block_place(down_col[0]), down_local[0])
    up4, down4 = up_perm.reshape(-1, HPD), down_perm.reshape(-1, HPD)
    wanted = jnp.stack([down4, up4 + 256], axis=1).reshape(-1)
    present = jnp.stack([up4, down4 + 256], axis=1).reshape(-1)
    route = (wanted[:, None] == present[None, :]).astype(BF)
    z_from_me = (jnp.arange(NZ) - lax.axis_index("tensor")) % NZ
    z_slot = jnp.sum(jnp.where(z_from_me[:, None] == jnp.arange(NZ), Z_SLOT[None], 0), axis=1)

    up_dense, down_dense = spread_weights(tables, pairs)
    sent, slope = forward(features, up_dense, down_dense)
    routed = jnp.dot(route, exchange(sent), preferred_element_type=F32).astype(BF)
    back = exchange(routed)
    me = lax.axis_index("dp").astype(jnp.int32).reshape(1)
    slots, dpre = weight_terms(tables, features, back, slope)
    return reduce_all(me, slots, *input_terms(z_slot.astype(jnp.int32), dpre, up_dense))


def solution(mesh):
    return jax.shard_map(
        per_device,
        mesh=mesh,
        in_specs=(
            P("dp", "tensor"),
            P("dp", "tensor"),
            P("tensor", "dp", None),
            P("tensor", "dp", None),
            P("tensor", None),
            P("tensor", None),
            P("tensor", None),
            P("tensor", None),
            P(),
            P(),
        ),
        out_specs=(P("dp", "tensor"), P("tensor", None, None), P("tensor", None, None)),
        check_vma=False,
    )
```
